256 devices in a mesh: batch: 4 (over y_hi, core), field: 64 (over z, x, y_lo).
Axes of the slice: x: 4, y: 4 (y_hi: 2, y_lo: 2; y = y_hi * 2 + y_lo), z: 8, core: 2. Of those that a mesh axis runs over, the one named last changes fastest.
Arguments:
- vectors: bfloat16 [4096, 128, 128, 8], P('batch', 'field'), may hold values from -6 to 6
- first_weight: bfloat16 [128, 64, 8, 512], P('field'), may hold values from -0.0234375 to 0.0234375
- second_weight: bfloat16 [512, 256], replicated, may hold values from -0.25 to 0.25
- out_weight: float32 [256], replicated, may hold values from -0.375 to 0.375
- upstream: float32 [4096], P('batch'), may hold values from -6 to 6
Outputs:
- logits: float32 [4096], P('batch')
- grad_vectors: float32 [4096, 128, 128, 8], P('batch', 'field')
- grad_first: float32 [128, 64, 8, 512], P('field', 'batch')
- grad_second: float32 [512, 256], replicated
- grad_out: float32 [256], replicated
The draws below stay inside these ranges and needn't reach their ends.
All inputs are finite; a program needn't handle non-finite values.
Results may differ from the reference program's by a relative error of at most 0.0067.
Values may be sent and summed in bfloat16 or wider, within the bound.
No kernel may reach another device: no remote copies, remote signals or barrier semaphores. Data moves between devices by JAX's collectives and lax.ppermute only.
A program may use at most 128 MiB of HBM per device.

```python
import jax
import jax.numpy as jnp
from jax import lax

F = 128
K = 8
H = 512
H2 = 256
BATCH = 4096
SLOTS = 64


def levels(key, shape, shards, least, high):
    def one(axis_at, parts):
        draws = jax.random.uniform(jax.random.fold_in(jax.random.fold_in(key, 6), axis_at), (parts,), jnp.float32, least / len(shards), high / len(shards))
        return jnp.repeat(jnp.exp(draws), shape[axis_at] // parts).reshape((-1,) + (1,) * (len(shape) - axis_at - 1))

    loudness = one(*shards[0])
    for cut in shards[1:]:
        loudness = loudness * one(*cut)
    return loudness


def gaussian(stream_key, shape, width, most, shards=(), held_as=jnp.bfloat16):
    level = levels(stream_key, shape, shards, -0.22, 0.18) if shards else 1.0
    drawn = jax.random.normal(stream_key, shape, jnp.float32) * width * level
    return jnp.minimum(jnp.maximum(drawn, -most), most).astype(held_as)


def setup_inputs(seed: int = 0) -> dict:
    key_of = jax.random.split(jax.random.key(seed), 6)
    vectors = gaussian(key_of[0], (BATCH, F, F, K), 1.0, 6.0, ((0, 4), (1, 64)))
    first_weight = gaussian(key_of[1], (F, SLOTS, K, H), (F * K * (F - 1) // 2) ** -0.5, 0.0234375, ((0, 64),))
    second_weight = gaussian(key_of[2], (H, H2), H ** -0.5, 0.25)
    out_weight = gaussian(key_of[3], (H2,), H2 ** -0.5, 0.375, (), jnp.float32)
    upstream = gaussian(key_of[4], (BATCH,), 1.0, 6.0, ((0, 4),), jnp.float32)
    return {"vectors": vectors, "first_weight": first_weight, "second_weight": second_weight, "out_weight": out_weight, "upstream": upstream}


def silu_slope(value):
    sigmoid_value = jax.nn.sigmoid(value)
    return sigmoid_value * (1.0 + value * (1.0 - sigmoid_value))


def dense_head(hidden, second_weight, out_weight, upstream):
    activated = jax.nn.silu(hidden).astype(jnp.bfloat16)
    second_pre = jnp.dot(activated, second_weight, preferred_element_type=jnp.float32)
    second_act = jax.nn.silu(second_pre)
    logits = jnp.dot(second_act, out_weight, precision=lax.Precision.HIGHEST)
    grad_pre = (upstream[:, None] * out_weight[None, :] * silu_slope(second_pre)).astype(jnp.bfloat16)
    grad_second = lax.dot_general(activated, grad_pre, (((0,), (0,)), ((), ())), preferred_element_type=jnp.float32)
    grad_out = lax.dot_general(second_act, upstream, (((0,), (0,)), ((), ())), precision=lax.Precision.HIGHEST)
    back_hidden = lax.dot_general(grad_pre, second_weight, (((1,), (1,)), ((), ())), preferred_element_type=jnp.float32)
    grad_hidden = (back_hidden * silu_slope(hidden)).astype(jnp.bfloat16)
    return logits, grad_second, grad_out, grad_hidden


def reference(vectors, first_weight, second_weight, out_weight, upstream):
    block_rows = 64
    blocks = BATCH // block_rows
    half = F // 2
    field_index = jnp.arange(F, dtype=jnp.int32)
    slot_index = jnp.arange(half, dtype=jnp.int32)
    odd_field = (field_index % 2 == 1)[:, None]
    lower_slot = slot_index[None, :] <= (field_index // 2)[:, None]
    parity = jnp.logical_xor(odd_field, lower_slot)
    invalid = jnp.logical_and(jnp.logical_not(odd_field), slot_index[None, :] == (field_index // 2)[:, None])
    valid_mask = jnp.where(invalid, 0.0, 1.0).astype(jnp.float32)[None, :, :, None]
    parity_sel = parity[None, :, :, None]
    weights_flat = first_weight.reshape(F * half * K, H)
    grouped = vectors.reshape(blocks, block_rows, F, F, K)

    def select(full):
        split = full.reshape(block_rows, F, half, 2, K)
        return jnp.where(parity_sel, split[:, :, :, 1], split[:, :, :, 0])

    def place(slotted):
        zeros = jnp.zeros_like(slotted)
        stacked = jnp.stack([jnp.where(parity_sel, zeros, slotted), jnp.where(parity_sel, slotted, zeros)], axis=3)
        return stacked.reshape(block_rows, F, F, K)

    def make_pairs(block):
        values = block.astype(jnp.float32)
        own = select(values)
        other = select(jnp.transpose(values, (0, 2, 1, 3)))
        return (own * other * valid_mask).astype(jnp.bfloat16), own, other

    def forward(block):
        pairs, own, other = make_pairs(block)
        return jnp.dot(pairs.reshape(block_rows, -1), weights_flat, preferred_element_type=jnp.float32)

    hidden = lax.map(forward, grouped).reshape(BATCH, H)
    logits, grad_second, grad_out, grad_hidden = dense_head(hidden, second_weight, out_weight, upstream)
    grad_grouped = grad_hidden.reshape(blocks, block_rows, H)

    def backward(total, items):
        block, grad_block = items
        pairs, own, other = make_pairs(block)
        total = total + lax.dot_general(pairs.reshape(block_rows, -1), grad_block, (((0,), (0,)), ((), ())), preferred_element_type=jnp.float32)
        grad_pairs = lax.dot_general(grad_block, weights_flat, (((1,), (1,)), ((), ())), preferred_element_type=jnp.float32)
        grad_pairs = grad_pairs.reshape(block_rows, F, half, K) * valid_mask
        returning = lax.optimization_barrier((grad_pairs * own).astype(jnp.bfloat16))
        own_full = place(grad_pairs * other)
        back_full = jnp.transpose(place(returning.astype(jnp.float32)), (0, 2, 1, 3))
        return total, own_full + back_full

    grad_flat, grad_vectors = lax.scan(backward, jnp.zeros((F * half * K, H), jnp.float32), (grouped, grad_grouped))
    grad_vectors = grad_vectors.reshape(BATCH, F, F, K)
    grad_first = grad_flat.reshape(F, half, K, H)
    return logits, grad_vectors, grad_first, grad_second, grad_out
```

```python
import jax
import jax.numpy as jnp
from jax import lax
from jax.sharding import PartitionSpec as P


def silu_slope(value):
    sigmoid_value = jax.nn.sigmoid(value)
    return sigmoid_value * (1.0 + value * (1.0 - sigmoid_value))


def dense_head(hidden, second_weight, out_weight, upstream):
    activated = jax.nn.silu(hidden).astype(jnp.bfloat16)
    second_pre = jnp.dot(activated, second_weight, preferred_element_type=jnp.float32)
    second_act = jax.nn.silu(second_pre)
    logits = jnp.dot(second_act, out_weight, precision=lax.Precision.HIGHEST)
    grad_pre = (upstream[:, None] * out_weight[None, :] * silu_slope(second_pre)).astype(
        jnp.bfloat16
    )
    grad_second = lax.dot_general(
        activated, grad_pre, (((0,), (0,)), ((), ())), preferred_element_type=jnp.float32
    )
    grad_out = lax.dot_general(
        second_act, upstream, (((0,), (0,)), ((), ())), precision=lax.Precision.HIGHEST
    )
    back_hidden = lax.dot_general(
        grad_pre, second_weight, (((1,), (1,)), ((), ())), preferred_element_type=jnp.float32
    )
    grad_hidden = (back_hidden * silu_slope(hidden)).astype(jnp.bfloat16)
    return (logits, grad_second, grad_out, grad_hidden)


PLANE = 8


def inner_groups(owners):
    return [[base + at for at in range(PLANE)] for base in range(0, owners, PLANE)]


def outer_groups(owners):
    return [[base + at for base in range(0, owners, PLANE)] for at in range(PLANE)]


def exchange(blocks, groups):
    return lax.all_to_all(blocks, "field", 0, 0, axis_index_groups=groups, tiled=True)


def field_sum(partial):
    owners = lax.axis_size("field")
    inner, outer = inner_groups(owners), outer_groups(owners)
    depth = owners // PLANE
    rows, width = partial.shape
    blocks = partial.astype(jnp.bfloat16).reshape(PLANE, rows // PLANE, width)
    share = jnp.sum(exchange(blocks, inner).astype(jnp.float32), axis=0)
    blocks = share.astype(jnp.bfloat16).reshape(depth, rows // owners, width)
    share = jnp.sum(exchange(blocks, outer).astype(jnp.float32), axis=0)
    share = share.astype(jnp.bfloat16)
    copies = jnp.broadcast_to(share[None], (depth,) + share.shape)
    plane = exchange(copies, outer).reshape(rows // PLANE, width)
    copies = jnp.broadcast_to(plane[None], (PLANE,) + plane.shape)
    return exchange(copies, inner).reshape(rows, width).astype(jnp.float32)


CORE_PAIRS = [(0, 1), (1, 0), (2, 3), (3, 2)]
FAR_PAIRS = [(0, 2), (2, 0), (1, 3), (3, 1)]


def batch_sum(value):
    value = value + lax.ppermute(value, "batch", CORE_PAIRS)
    return value + lax.ppermute(value, "batch", FAR_PAIRS)


def batch_scatter(value):
    place = lax.axis_index("batch")
    far, core = place // 2, place % 2
    split = value.reshape((2, 2, value.shape[0] // 4) + value.shape[1:])
    keep = lax.dynamic_index_in_dim(split, core, 1, keepdims=False)
    give = lax.dynamic_index_in_dim(split, 1 - core, 1, keepdims=False)
    split = keep + lax.ppermute(give, "batch", CORE_PAIRS)
    keep = lax.dynamic_index_in_dim(split, far, 0, keepdims=False)
    give = lax.dynamic_index_in_dim(split, 1 - far, 0, keepdims=False)
    return keep + lax.ppermute(give, "batch", FAR_PAIRS)


def per_device(vectors, first_weight, second_weight, out_weight, upstream):
    row_count, local_fields, field_total, latent = vectors.shape
    hidden_width = first_weight.shape[3]
    half = field_total // 2
    owners = lax.axis_size("field")
    local_half = local_fields // 2
    mine = lax.axis_index("field")
    field_global = mine * local_fields + jnp.arange(local_fields, dtype=jnp.int32)
    slot_index = jnp.arange(half, dtype=jnp.int32)
    odd_field = (field_global % 2 == 1)[:, None]
    lower_slot = slot_index[None, :] <= (field_global // 2)[:, None]
    parity_own = jnp.logical_xor(odd_field, lower_slot)[None, :, :, None]
    invalid = jnp.logical_and(
        jnp.logical_not(odd_field), slot_index[None, :] == (field_global // 2)[:, None]
    )
    valid_mask = jnp.where(invalid, 0.0, 1.0).astype(jnp.float32)[None, :, :, None]
    split_own = vectors.reshape(row_count, local_fields, half, 2, latent)
    own = jnp.where(parity_own, split_own[:, :, :, 1], split_own[:, :, :, 0])
    sender_slot = jnp.arange(local_half, dtype=jnp.int32)[:, None, None]
    target_owner = jnp.arange(owners, dtype=jnp.int32)[None, :, None]
    target_field = jnp.arange(local_fields, dtype=jnp.int32)[None, None, :]
    earlier = mine * local_half + sender_slot <= target_owner * local_half + target_field // 2
    parity_send = jnp.logical_xor(target_field % 2 == 1, earlier)[None, :, :, :, None]
    split_send = vectors.reshape(row_count, local_half, 2, owners, local_fields, latent)
    outgoing = jnp.where(parity_send, split_send[:, :, 1], split_send[:, :, 0])
    outgoing = jnp.transpose(outgoing, (0, 3, 2, 1, 4))
    received = lax.all_to_all(outgoing, "field", split_axis=2, concat_axis=2, tiled=True)
    other = received.reshape(row_count, local_fields, half, latent)
    own_float = own.astype(jnp.float32)
    other_float = other.astype(jnp.float32)
    pairs = (own_float * other_float * valid_mask).astype(jnp.bfloat16)
    weights_flat = first_weight.reshape(-1, hidden_width)
    partial_value = jnp.dot(
        pairs.reshape(row_count, -1), weights_flat, preferred_element_type=jnp.float32
    )
    hidden = field_sum(partial_value)
    logits, grad_second, grad_out, grad_hidden = dense_head(
        hidden, second_weight, out_weight, upstream
    )
    grad_second = batch_sum(grad_second)
    grad_out = batch_sum(grad_out)
    grad_share_first = batch_scatter(
        jnp.einsum("bcmk,bh->mckh", pairs, grad_hidden, preferred_element_type=jnp.float32)
    )
    grad_first = jnp.transpose(grad_share_first, (1, 0, 2, 3))
    grad_pairs = lax.dot_general(
        grad_hidden, weights_flat, (((1,), (1,)), ((), ())), preferred_element_type=jnp.float32
    )
    grad_pairs = grad_pairs.reshape(row_count, local_fields, half, latent) * valid_mask
    own_grads = grad_pairs * other_float
    zeros_own = jnp.zeros_like(own_grads)
    own_full = jnp.stack(
        [jnp.where(parity_own, zeros_own, own_grads), jnp.where(parity_own, own_grads, zeros_own)],
        axis=3,
    )
    own_full = own_full.reshape(row_count, local_fields, field_total, latent)
    returning = (grad_pairs * own_float).astype(jnp.bfloat16)
    returning = returning.reshape(row_count, local_fields, owners, local_half, latent)
    arrived = lax.all_to_all(returning, "field", split_axis=2, concat_axis=2, tiled=True)
    arrived = jnp.transpose(arrived.astype(jnp.float32), (0, 3, 2, 1, 4))
    zeros_back = jnp.zeros_like(arrived)
    back_full = jnp.stack(
        [jnp.where(parity_send, zeros_back, arrived), jnp.where(parity_send, arrived, zeros_back)],
        axis=2,
    )
    back_full = back_full.reshape(row_count, local_fields, field_total, latent)
    grad_vectors = own_full + back_full
    return (logits, grad_vectors, grad_first, grad_second, grad_out)


def solution(mesh):
    return jax.shard_map(
        per_device,
        mesh=mesh,
        in_specs=(
            P("batch", "field", None, None),
            P("field", None, None, None),
            P(),
            P(),
            P("batch"),
        ),
        out_specs=(
            P("batch"),
            P("batch", "field", None, None),
            P("field", "batch", None, None),
            P(),
            P(),
        ),
        check_vma=False,
    )
```

```python
import jax
import jax.numpy as jnp
from jax import lax
from jax.experimental import pallas as pl
from jax.experimental.pallas import tpu as pltpu
from jax.sharding import PartitionSpec as P

PLANE = 8
LANES = 128
TURN = 512
MIB = 1024 * 1024
CORE_PAIRS = [(0, 1), (1, 0), (2, 3), (3, 2)]
FAR_PAIRS = [(0, 2), (2, 0), (1, 3), (3, 1)]
NT = (((1,), (1,)), ((), ()))


def silu_slope(value):
    sigmoid_value = jax.nn.sigmoid(value)
    return sigmoid_value * (1.0 + value * (1.0 - sigmoid_value))


def params(mib):
    return pltpu.CompilerParams(vmem_limit_bytes=mib * MIB)


def cost(flops, moved):
    return pl.CostEstimate(flops=flops, bytes_accessed=moved, transcendentals=0)


SMEM_SPEC = pl.BlockSpec(memory_space=pltpu.SMEM)


def lane_owner(shape):
    lane = lax.broadcasted_iota(jnp.int32, shape, len(shape) - 1)
    return lane // 2, lane % 2


def own_field(owner, parity, mine):
    return jnp.where(owner <= mine, 1 - parity, parity)


def sent_field(owner, parity, mine):
    return jnp.where(owner >= mine, 1 - parity, parity)


def turn_out(chosen, planes_ref, turned_ref):
    rows, latent, lanes = chosen.shape
    planes_ref[...] = chosen.reshape(rows * latent, lanes)
    for k in range(latent):
        plane = planes_ref[pl.ds(k, rows, stride=latent), :]
        turned_ref[pl.ds(k, lanes, stride=latent), :] = plane.T


def send_part(mine_ref, vectors_ref, send_ref, planes_ref, turned_ref):
    rows, _, latent, lanes = vectors_ref.shape
    owner, parity = lane_owner((1, latent, lanes))
    field = sent_field(owner, parity, mine_ref[0])
    chosen = jnp.where(
        field == 1, vectors_ref[:, 1].astype(jnp.float32), vectors_ref[:, 0].astype(jnp.float32)
    )
    turn_out(chosen, planes_ref, turned_ref)
    send_ref[...] = turned_ref[...].astype(jnp.bfloat16).reshape(send_ref.shape)


def own_part(mine_ref, vectors_ref, own_ref, planes_ref, turned_ref):
    rows, _, latent, lanes = vectors_ref.shape
    half = lanes // 2
    owner, parity = lane_owner((1, latent, lanes))
    field = own_field(owner, parity, mine_ref[0])
    chosen = jnp.where(
        field == 1, vectors_ref[:, 1].astype(jnp.float32), vectors_ref[:, 0].astype(jnp.float32)
    )
    turn_out(chosen, planes_ref, turned_ref)
    turned = turned_ref[...].reshape(half, 2, latent, rows)
    low = lax.broadcasted_iota(jnp.int32, (half, latent, rows), 0) <= mine_ref[0]
    even, odd = turned[:, 0], turned[:, 1]
    own_ref[0] = jnp.where(low, odd, even).astype(jnp.bfloat16).reshape(half * latent, rows)
    own_ref[1] = jnp.where(low, even, odd).astype(jnp.bfloat16).reshape(half * latent, rows)


def pieces(rows):
    return [pl.ds(at, min(rows, LANES)) for at in range(0, rows, LANES)]


def send_kernel(mine_ref, vectors_ref, send_ref, *scratch):
    for piece in pieces(vectors_ref.shape[0]):
        send_part(mine_ref, vectors_ref.at[piece], send_ref.at[:, :, piece], *scratch)


def own_kernel(mine_ref, vectors_ref, own_ref, *scratch):
    for piece in pieces(vectors_ref.shape[0]):
        own_part(mine_ref, vectors_ref.at[piece], own_ref.at[:, :, piece], *scratch)


def turn_call(kernel, mine, vectors, out_shape, out_block, out_map, block):
    rows, local_fields, latent, lanes = vectors.shape
    return pl.pallas_call(
        kernel,
        grid=(rows // block,),
        in_specs=[
            SMEM_SPEC,
            pl.BlockSpec((block, local_fields, latent, lanes), lambda at: (at, 0, 0, 0)),
        ],
        out_specs=pl.BlockSpec(out_block, out_map),
        out_shape=jax.ShapeDtypeStruct(out_shape, jnp.bfloat16),
        scratch_shapes=turn_scratch(block, latent, lanes),
        compiler_params=params(48),
        cost_estimate=cost(0, vectors.size * 3),
    )(mine, vectors)


def make_send(mine, vectors):
    rows, _, latent, lanes = vectors.shape
    owners, block = lanes // 2, min(rows, TURN)
    return turn_call(
        send_kernel,
        mine,
        vectors,
        (owners, 2 * latent, rows),
        (owners, 2 * latent, block),
        lambda at: (0, 0, at),
        block,
    )


def make_own(mine, vectors):
    rows, _, latent, lanes = vectors.shape
    half, block = lanes // 2, min(rows, TURN)
    return turn_call(
        own_kernel,
        mine,
        vectors,
        (2, half * latent, rows),
        (2, half * latent, block),
        lambda at: (0, 0, at),
        block,
    )


def pairs_kernel(mine_ref, own_ref, other_ref, weights_ref, pairs_ref, partial_ref):
    half = other_ref.shape[0]
    rows = other_ref.shape[2]
    latent = own_ref.shape[1] // half
    total = None
    others = other_ref[...].astype(jnp.float32).reshape(half, 2, latent, rows)
    for i in range(2):
        own = own_ref[i].astype(jnp.float32).reshape(half, latent, rows)
        product = own * others[:, i]
        if i == 0:
            slot = lax.broadcasted_iota(jnp.int32, product.shape, 0)
            product = jnp.where(slot == mine_ref[0], 0.0, product)
        product = product.astype(jnp.bfloat16).reshape(half * latent, rows)
        pairs_ref[i] = product
        part = jnp.dot(weights_ref[i], product, preferred_element_type=jnp.float32)
        total = part if total is None else total + part
    partial_ref[...] = total.astype(jnp.bfloat16)


def make_pairs(mine, own, other, weights_turned):
    _, depth, rows = own.shape
    owners, wide, _ = other.shape
    width = weights_turned.shape[1]
    block = min(rows, 512)
    return pl.pallas_call(
        pairs_kernel,
        grid=(rows // block,),
        in_specs=[
            SMEM_SPEC,
            pl.BlockSpec((2, depth, block), lambda at: (0, 0, at)),
            pl.BlockSpec((owners, wide, block), lambda at: (0, 0, at)),
            pl.BlockSpec((2, width, depth), lambda at: (0, 0, 0)),
        ],
        out_specs=[
            pl.BlockSpec((2, depth, block), lambda at: (0, 0, at)),
            pl.BlockSpec((width, block), lambda at: (0, at)),
        ],
        out_shape=[
            jax.ShapeDtypeStruct((2, depth, rows), jnp.bfloat16),
            jax.ShapeDtypeStruct((width, rows), jnp.bfloat16),
        ],
        compiler_params=params(48),
        cost_estimate=cost(4 * depth * rows * width, 16 * depth * rows),
    )(mine, own, other, weights_turned)


def head_kernel(
    mine_ref,
    hidden_ref,
    second_ref,
    second_turned_ref,
    out_weight_ref,
    upstream_ref,
    weights_ref,
    own_ref,
    logits_ref,
    grad_second_ref,
    grad_out_ref,
    grad_hidden_ref,
    returning_ref,
):
    half = returning_ref.shape[0]
    rows = returning_ref.shape[2]
    latent = own_ref.shape[1] // half
    hidden = hidden_ref[...].astype(jnp.float32)
    sigmoid_hidden = jax.nn.sigmoid(hidden)
    activated = (hidden * sigmoid_hidden).astype(jnp.bfloat16)
    second_pre = jnp.dot(second_turned_ref[...], activated, preferred_element_type=jnp.float32)
    sigmoid_pre = jax.nn.sigmoid(second_pre)
    second_act = second_pre * sigmoid_pre
    out_weight = out_weight_ref[...]
    upstream = upstream_ref[...]
    logits_ref[...] = jnp.sum(second_act * out_weight, axis=0, keepdims=True)
    slope = sigmoid_pre * (1.0 + second_pre * (1.0 - sigmoid_pre))
    grad_pre = (upstream * out_weight * slope).astype(jnp.bfloat16)
    grad_second = lax.dot_general(activated, grad_pre, NT, preferred_element_type=jnp.float32)
    grad_out = jnp.sum(second_act * upstream, axis=1, keepdims=True)

    @pl.when(pl.program_id(0) == 0)
    def _():
        grad_second_ref[...] = grad_second
        grad_out_ref[...] = grad_out

    @pl.when(pl.program_id(0) != 0)
    def _():
        grad_second_ref[...] += grad_second
        grad_out_ref[...] += grad_out

    back_hidden = jnp.dot(second_ref[...], grad_pre, preferred_element_type=jnp.float32)
    slope = sigmoid_hidden * (1.0 + hidden * (1.0 - sigmoid_hidden))
    grad_hidden = (back_hidden * slope).astype(jnp.bfloat16)
    grad_hidden_ref[...] = grad_hidden
    returning = []
    for i in range(2):
        grads = jnp.dot(weights_ref[i], grad_hidden, preferred_element_type=jnp.float32)
        grads = grads.reshape(half, latent, rows)
        if i == 0:
            slot = lax.broadcasted_iota(jnp.int32, grads.shape, 0)
            grads = jnp.where(slot == mine_ref[0], 0.0, grads)
        own = own_ref[i].astype(jnp.float32).reshape(half, latent, rows)
        returning.append(grads * own)
    returning = jnp.stack(returning, axis=1).reshape(returning_ref.shape)
    returning_ref[...] = returning.astype(jnp.bfloat16)


def run_head(mine, hidden, second, out_weight, upstream, weights, own, latent):
    width, rows = hidden.shape
    _, depth, _ = own.shape
    owners, wide = depth // latent, 2 * latent
    width_two = second.shape[1]
    block = min(rows, 1024)
    moved = lambda at: (0, 0, at)
    fixed = lambda at: (0, 0)
    return pl.pallas_call(
        head_kernel,
        grid=(rows // block,),
        in_specs=[
            SMEM_SPEC,
            pl.BlockSpec((width, block), lambda at: (0, at)),
            pl.BlockSpec((width, width_two), fixed),
            pl.BlockSpec((width_two, width), fixed),
            pl.BlockSpec((width_two, 1), fixed),
            pl.BlockSpec((1, block), lambda at: (0, at)),
            pl.BlockSpec((2, depth, width), lambda at: (0, 0, 0)),
            pl.BlockSpec((2, depth, block), moved),
        ],
        out_specs=[
            pl.BlockSpec((1, block), lambda at: (0, at)),
            pl.BlockSpec((width, width_two), fixed),
            pl.BlockSpec((width_two, 1), fixed),
            pl.BlockSpec((width, block), lambda at: (0, at)),
            pl.BlockSpec((owners, wide, block), moved),
        ],
        out_shape=[
            jax.ShapeDtypeStruct((1, rows), jnp.float32),
            jax.ShapeDtypeStruct((width, width_two), jnp.float32),
            jax.ShapeDtypeStruct((width_two, 1), jnp.float32),
            jax.ShapeDtypeStruct((width, rows), jnp.bfloat16),
            jax.ShapeDtypeStruct((owners, wide, rows), jnp.bfloat16),
        ],
        compiler_params=params(48),
        cost_estimate=cost(4 * depth * rows * width, 24 * depth * rows),
    )(
        mine,
        hidden,
        second,
        second.T,
        out_weight.reshape(width_two, 1),
        upstream.reshape(1, rows),
        weights,
        own,
    )


def turn_back(rows, latent, lanes, turned_ref, planes_ref):
    for k in range(latent):
        plane = turned_ref[pl.ds(k, lanes, stride=latent), :]
        planes_ref[pl.ds(k, rows, stride=latent), :] = plane.T
    return planes_ref[...].reshape(rows, latent, lanes)


def own_back_part(
    mine_ref, weights_ref, grad_hidden_ref, other_ref, back_ref, planes_ref, turned_ref
):
    rows, latent, lanes = back_ref.shape
    half = lanes // 2
    shape = (half, latent, rows)
    slot = lax.broadcasted_iota(jnp.int32, shape, 0)
    low = slot <= mine_ref[0]
    others = other_ref[...].astype(jnp.float32).reshape(half, 2, latent, rows)
    grad_hidden = grad_hidden_ref[...]
    first = jnp.dot(weights_ref[0], grad_hidden, preferred_element_type=jnp.float32)
    first = jnp.where(slot == mine_ref[0], 0.0, first.reshape(shape) * others[:, 0])
    second = jnp.dot(weights_ref[1], grad_hidden, preferred_element_type=jnp.float32)
    second = second.reshape(shape) * others[:, 1]
    turned = jnp.stack([jnp.where(low, second, first), jnp.where(low, first, second)], axis=1)
    turned_ref[...] = turned.reshape(lanes * latent, rows)
    back_ref[...] = turn_back(rows, latent, lanes, turned_ref, planes_ref)


def final_part(mine_ref, back_ref, arrived_ref, grads_ref, planes_ref, turned_ref):
    rows, latent, lanes = back_ref.shape
    turned_ref[...] = arrived_ref[...].astype(jnp.float32).reshape(lanes * latent, rows)
    arrived = turn_back(rows, latent, lanes, turned_ref, planes_ref)
    owner, parity = lane_owner((1, latent, lanes))
    kept = own_field(owner, parity, mine_ref[0])
    came = sent_field(owner, parity, mine_ref[0])
    own = back_ref[...]
    for f in range(2):
        grads_ref[:, f] = jnp.where(kept == f, own, 0.0) + jnp.where(came == f, arrived, 0.0)


def own_back_kernel(mine_ref, weights_ref, grad_hidden_ref, other_ref, back_ref, *scratch):
    for piece in pieces(back_ref.shape[0]):
        own_back_part(
            mine_ref,
            weights_ref,
            grad_hidden_ref.at[:, piece],
            other_ref.at[:, :, piece],
            back_ref.at[piece],
            *scratch,
        )


def final_kernel(mine_ref, back_ref, arrived_ref, grads_ref, *scratch):
    for piece in pieces(back_ref.shape[0]):
        final_part(
            mine_ref,
            back_ref.at[piece],
            arrived_ref.at[:, :, piece],
            grads_ref.at[piece],
            *scratch,
        )


def turn_scratch(block, latent, lanes):
    block = min(block, LANES)
    return [
        pltpu.VMEM((block * latent, lanes), jnp.float32),
        pltpu.VMEM((lanes * latent, block), jnp.float32),
    ]


def turn_own_grads(mine, weights, grad_hidden, other):
    width, rows = grad_hidden.shape
    owners, wide, _ = other.shape
    latent, lanes, block = wide // 2, 2 * owners, min(rows, TURN)
    return pl.pallas_call(
        own_back_kernel,
        grid=(rows // block,),
        in_specs=[
            SMEM_SPEC,
            pl.BlockSpec(weights.shape, lambda at: (0, 0, 0)),
            pl.BlockSpec((width, block), lambda at: (0, at)),
            pl.BlockSpec((owners, wide, block), lambda at: (0, 0, at)),
        ],
        out_specs=pl.BlockSpec((block, latent, lanes), lambda at: (at, 0, 0)),
        out_shape=jax.ShapeDtypeStruct((rows, latent, lanes), jnp.float32),
        scratch_shapes=turn_scratch(block, latent, lanes),
        compiler_params=params(48),
        cost_estimate=cost(2 * weights.size * rows, other.size * 6),
    )(mine, weights, grad_hidden, other)


def join_grads(mine, back, arrived):
    rows, latent, lanes = back.shape
    owners, wide, _ = arrived.shape
    block = min(rows, TURN)
    return pl.pallas_call(
        final_kernel,
        grid=(rows // block,),
        in_specs=[
            SMEM_SPEC,
            pl.BlockSpec((block, latent, lanes), lambda at: (at, 0, 0)),
            pl.BlockSpec((owners, wide, block), lambda at: (0, 0, at)),
        ],
        out_specs=pl.BlockSpec((block, 2, latent, lanes), lambda at: (at, 0, 0, 0)),
        out_shape=jax.ShapeDtypeStruct((rows, 2, latent, lanes), jnp.float32),
        scratch_shapes=turn_scratch(block, latent, lanes),
        compiler_params=params(48),
        cost_estimate=cost(0, back.size * 14),
    )(mine, back, arrived)


def inner_groups(owners):
    return [[base + at for at in range(PLANE)] for base in range(0, owners, PLANE)]


def outer_groups(owners):
    return [[base + at for base in range(0, owners, PLANE)] for at in range(PLANE)]


def exchange(blocks, groups=None):
    return lax.all_to_all(blocks, "field", 0, 0, axis_index_groups=groups, tiled=True)


def field_sum(partial):
    owners = lax.axis_size("field")
    inner, outer = inner_groups(owners), outer_groups(owners)
    depth = owners // PLANE
    units, rows = partial.shape
    share = exchange(partial.reshape(PLANE, units // PLANE, rows), inner)
    share = jnp.sum(share.astype(jnp.float32), axis=0)
    share = exchange(share.reshape(depth, units // owners, rows), outer)
    share = jnp.sum(share, axis=0).astype(jnp.bfloat16)
    copies = jnp.broadcast_to(share[None], (depth,) + share.shape)
    plane = exchange(copies, outer).reshape(units // PLANE, rows)
    copies = jnp.broadcast_to(plane[None], (PLANE,) + plane.shape)
    return exchange(copies, inner).reshape(units, rows)


def swap(value, pairs):
    return lax.ppermute(value, "batch", pairs)


def part_of(value, index, axis):
    return lax.dynamic_index_in_dim(value, index, axis, keepdims=False)


def batch_sum(value):
    core = lax.axis_index("batch") % 2
    split = value.reshape((2, value.shape[0] // 2) + value.shape[1:])
    share = part_of(split, core, 0) + swap(part_of(split, 1 - core, 0), CORE_PAIRS)
    share = share + swap(share, FAR_PAIRS)
    mate = swap(share, CORE_PAIRS)
    first = jnp.where(core == 0, share, mate)
    second = jnp.where(core == 0, mate, share)
    return jnp.stack([first, second]).reshape(value.shape)


def batch_scatter(value):
    place = lax.axis_index("batch")
    far, core = place // 2, place % 2
    fields, slots = value.shape[:2]
    split = value.reshape((fields, 2, 2, slots // 4) + value.shape[2:])
    split = part_of(split, core, 2) + swap(part_of(split, 1 - core, 2), CORE_PAIRS)
    give = part_of(split, 1 - far, 1).astype(jnp.bfloat16)
    return part_of(split, far, 1) + swap(give, FAR_PAIRS).astype(jnp.float32)


def per_device(vectors, first_weight, second_weight, out_weight, upstream):
    local_fields, half, latent, width = first_weight.shape
    mine = lax.axis_index("field").astype(jnp.int32).reshape(1)
    turned = jnp.transpose(vectors, (0, 1, 3, 2))
    weights = first_weight.reshape(local_fields, half * latent, width)
    other = exchange(make_send(mine, turned))
    own = make_own(mine, turned)
    pairs, partial = make_pairs(mine, own, other, jnp.transpose(weights, (0, 2, 1)))
    hidden = field_sum(partial)
    logits, grad_second, grad_out, grad_hidden, returning = run_head(
        mine, hidden, second_weight, out_weight, upstream, weights, own, latent
    )
    arrived = exchange(returning)
    grad_share = lax.dot_general(
        pairs.reshape(-1, pairs.shape[2]), grad_hidden, NT, preferred_element_type=jnp.float32
    )
    grad_first = batch_scatter(grad_share.reshape(first_weight.shape))
    grad_second = batch_sum(grad_second)
    grad_out = batch_sum(grad_out.reshape(-1))
    back = turn_own_grads(mine, weights, grad_hidden, other)
    grad_vectors = jnp.transpose(join_grads(mine, back, arrived), (0, 1, 3, 2))
    return (logits.reshape(-1), grad_vectors, grad_first, grad_second, grad_out)


def solution(mesh):
    return jax.shard_map(
        per_device,
        mesh=mesh,
        in_specs=(
            P("batch", "field", None, None),
            P("field", None, None, None),
            P(),
            P(),
            P("batch"),
        ),
        out_specs=(
            P("batch"),
            P("batch", "field", None, None),
            P("field", "batch", None, None),
            P(),
            P(),
        ),
        check_vma=False,
    )
```

```python
import jax
import jax.numpy as jnp
from jax import lax
from jax.experimental import pallas as pl
from jax.experimental.pallas import tpu as pltpu
from jax.sharding import PartitionSpec as P

PLANE = 8
LANES = 128
TURN = 512
MIB = 1024 * 1024
CORE_PAIRS = [(0, 1), (1, 0), (2, 3), (3, 2)]
FAR_PAIRS = [(0, 2), (2, 0), (1, 3), (3, 1)]
NT = (((1,), (1,)), ((), ()))


def silu_slope(value):
    sigmoid_value = jax.nn.sigmoid(value)
    return sigmoid_value * (1.0 + value * (1.0 - sigmoid_value))


def params(mib):
    return pltpu.CompilerParams(vmem_limit_bytes=mib * MIB)


def cost(flops, moved):
    return pl.CostEstimate(flops=flops, bytes_accessed=moved, transcendentals=0)


SMEM_SPEC = pl.BlockSpec(memory_space=pltpu.SMEM)


def lane_owner(shape):
    lane = lax.broadcasted_iota(jnp.int32, shape, len(shape) - 1)
    return lane // 2, lane % 2


def own_field(owner, parity, mine):
    return jnp.where(owner <= mine, 1 - parity, parity)


def sent_field(owner, parity, mine):
    return jnp.where(owner >= mine, 1 - parity, parity)


def turn_out(chosen, planes_ref, turned_ref):
    rows, latent, lanes = chosen.shape
    planes_ref[...] = chosen.reshape(rows * latent, lanes)
    for k in range(latent):
        plane = planes_ref[pl.ds(k, rows, stride=latent), :]
        turned_ref[pl.ds(k, lanes, stride=latent), :] = plane.T


def send_part(mine_ref, vectors_ref, send_ref, planes_ref, turned_ref):
    rows, _, latent, lanes = vectors_ref.shape
    owner, parity = lane_owner((1, latent, lanes))
    field = sent_field(owner, parity, mine_ref[0])
    chosen = jnp.where(
        field == 1, vectors_ref[:, 1].astype(jnp.float32), vectors_ref[:, 0].astype(jnp.float32)
    )
    turn_out(chosen, planes_ref, turned_ref)
    send_ref[...] = turned_ref[...].astype(jnp.bfloat16).reshape(send_ref.shape)


def own_part(mine_ref, vectors_ref, own_ref, planes_ref, turned_ref):
    rows, _, latent, lanes = vectors_ref.shape
    half = lanes // 2
    owner, parity = lane_owner((1, latent, lanes))
    field = own_field(owner, parity, mine_ref[0])
    chosen = jnp.where(
        field == 1, vectors_ref[:, 1].astype(jnp.float32), vectors_ref[:, 0].astype(jnp.float32)
    )
    turn_out(chosen, planes_ref, turned_ref)
    turned = turned_ref[...].reshape(half, 2, latent, rows)
    low = lax.broadcasted_iota(jnp.int32, (half, latent, rows), 0) <= mine_ref[0]
    even, odd = turned[:, 0], turned[:, 1]
    own_ref[0] = jnp.where(low, odd, even).astype(jnp.bfloat16).reshape(half * latent, rows)
    own_ref[1] = jnp.where(low, even, odd).astype(jnp.bfloat16).reshape(half * latent, rows)


def pieces(rows):
    return [pl.ds(at, min(rows, LANES)) for at in range(0, rows, LANES)]


def send_kernel(mine_ref, vectors_ref, send_ref, *scratch):
    for piece in pieces(vectors_ref.shape[0]):
        send_part(mine_ref, vectors_ref.at[piece], send_ref.at[:, :, piece], *scratch)


def own_kernel(mine_ref, vectors_ref, own_ref, *scratch):
    for piece in pieces(vectors_ref.shape[0]):
        own_part(mine_ref, vectors_ref.at[piece], own_ref.at[:, :, piece], *scratch)


def turn_call(kernel, mine, vectors, out_shape, out_block, out_map, block):
    rows, local_fields, latent, lanes = vectors.shape
    return pl.pallas_call(
        kernel,
        grid=(rows // block,),
        in_specs=[
            SMEM_SPEC,
            pl.BlockSpec((block, local_fields, latent, lanes), lambda at: (at, 0, 0, 0)),
        ],
        out_specs=pl.BlockSpec(out_block, out_map),
        out_shape=jax.ShapeDtypeStruct(out_shape, jnp.bfloat16),
        scratch_shapes=turn_scratch(block, latent, lanes),
        compiler_params=params(60),
        cost_estimate=cost(0, vectors.size * 3),
    )(mine, vectors)


def make_send(mine, vectors):
    rows, _, latent, lanes = vectors.shape
    owners, block = lanes // 2, min(rows, TURN)
    return turn_call(
        send_kernel,
        mine,
        vectors,
        (owners, 2 * latent, rows),
        (owners, 2 * latent, block),
        lambda at: (0, 0, at),
        block,
    )


def make_own(mine, vectors):
    rows, _, latent, lanes = vectors.shape
    half, block = lanes // 2, min(rows, TURN)
    return turn_call(
        own_kernel,
        mine,
        vectors,
        (2, half * latent, rows),
        (2, half * latent, block),
        lambda at: (0, 0, at),
        block,
    )


def pairs_kernel(mine_ref, own_ref, other_ref, weights_ref, pairs_ref, partial_ref):
    half = other_ref.shape[0]
    rows = other_ref.shape[2]
    latent = own_ref.shape[1] // half
    total = None
    others = other_ref[...].astype(jnp.float32).reshape(half, 2, latent, rows)
    for i in range(2):
        own = own_ref[i].astype(jnp.float32).reshape(half, latent, rows)
        product = own * others[:, i]
        if i == 0:
            slot = lax.broadcasted_iota(jnp.int32, product.shape, 0)
            product = jnp.where(slot == mine_ref[0], 0.0, product)
        product = product.astype(jnp.bfloat16).reshape(half * latent, rows)
        pairs_ref[i] = product
        part = jnp.dot(weights_ref[i], product, preferred_element_type=jnp.float32)
        total = part if total is None else total + part
    partial_ref[...] = total.astype(jnp.bfloat16)


def make_pairs(mine, own, other, weights_turned):
    _, depth, rows = own.shape
    owners, wide, _ = other.shape
    width = weights_turned.shape[1]
    block = min(rows, 512)
    return pl.pallas_call(
        pairs_kernel,
        grid=(rows // block,),
        in_specs=[
            SMEM_SPEC,
            pl.BlockSpec((2, depth, block), lambda at: (0, 0, at)),
            pl.BlockSpec((owners, wide, block), lambda at: (0, 0, at)),
            pl.BlockSpec((2, width, depth), lambda at: (0, 0, 0)),
        ],
        out_specs=[
            pl.BlockSpec((2, depth, block), lambda at: (0, 0, at)),
            pl.BlockSpec((width, block), lambda at: (0, at)),
        ],
        out_shape=[
            jax.ShapeDtypeStruct((2, depth, rows), jnp.bfloat16),
            jax.ShapeDtypeStruct((width, rows), jnp.bfloat16),
        ],
        compiler_params=params(24),
        cost_estimate=cost(4 * depth * rows * width, 16 * depth * rows),
    )(mine, own, other, weights_turned)


def head_kernel(
    mine_ref,
    hidden_ref,
    second_ref,
    second_turned_ref,
    out_weight_ref,
    upstream_ref,
    weights_ref,
    own_ref,
    logits_ref,
    grad_second_ref,
    grad_out_ref,
    grad_hidden_ref,
    returning_ref,
):
    half = returning_ref.shape[0]
    rows = returning_ref.shape[2]
    latent = own_ref.shape[1] // half
    hidden = hidden_ref[...].astype(jnp.float32)
    sigmoid_hidden = jax.nn.sigmoid(hidden)
    activated = (hidden * sigmoid_hidden).astype(jnp.bfloat16)
    second_pre = jnp.dot(second_turned_ref[...], activated, preferred_element_type=jnp.float32)
    sigmoid_pre = jax.nn.sigmoid(second_pre)
    second_act = second_pre * sigmoid_pre
    out_weight = out_weight_ref[...]
    upstream = upstream_ref[...]
    logits_ref[...] = jnp.sum(second_act * out_weight, axis=0, keepdims=True)
    slope = sigmoid_pre * (1.0 + second_pre * (1.0 - sigmoid_pre))
    grad_pre = (upstream * out_weight * slope).astype(jnp.bfloat16)
    grad_second = lax.dot_general(activated, grad_pre, NT, preferred_element_type=jnp.float32)
    grad_out = jnp.sum(second_act * upstream, axis=1, keepdims=True)

    @pl.when(pl.program_id(0) == 0)
    def _():
        grad_second_ref[...] = grad_second
        grad_out_ref[...] = grad_out

    @pl.when(pl.program_id(0) != 0)
    def _():
        grad_second_ref[...] += grad_second
        grad_out_ref[...] += grad_out

    back_hidden = jnp.dot(second_ref[...], grad_pre, preferred_element_type=jnp.float32)
    slope = sigmoid_hidden * (1.0 + hidden * (1.0 - sigmoid_hidden))
    grad_hidden = (back_hidden * slope).astype(jnp.bfloat16)
    grad_hidden_ref[...] = grad_hidden
    returning = []
    for i in range(2):
        grads = jnp.dot(weights_ref[i], grad_hidden, preferred_element_type=jnp.float32)
        grads = grads.reshape(half, latent, rows)
        if i == 0:
            slot = lax.broadcasted_iota(jnp.int32, grads.shape, 0)
            grads = jnp.where(slot == mine_ref[0], 0.0, grads)
        own = own_ref[i].astype(jnp.float32).reshape(half, latent, rows)
        returning.append(grads * own)
    returning = jnp.stack(returning, axis=1).reshape(returning_ref.shape)
    returning_ref[...] = returning.astype(jnp.bfloat16)


def run_head(mine, hidden, second, out_weight, upstream, weights, own, latent):
    width, rows = hidden.shape
    _, depth, _ = own.shape
    owners, wide = depth // latent, 2 * latent
    width_two = second.shape[1]
    block = min(rows, 1024)
    moved = lambda at: (0, 0, at)
    fixed = lambda at: (0, 0)
    return pl.pallas_call(
        head_kernel,
        grid=(rows // block,),
        in_specs=[
            SMEM_SPEC,
            pl.BlockSpec((width, block), lambda at: (0, at)),
            pl.BlockSpec((width, width_two), fixed),
            pl.BlockSpec((width_two, width), fixed),
            pl.BlockSpec((width_two, 1), fixed),
            pl.BlockSpec((1, block), lambda at: (0, at)),
            pl.BlockSpec((2, depth, width), lambda at: (0, 0, 0)),
            pl.BlockSpec((2, depth, block), moved),
        ],
        out_specs=[
            pl.BlockSpec((1, block), lambda at: (0, at)),
            pl.BlockSpec((width, width_two), fixed),
            pl.BlockSpec((width_two, 1), fixed),
            pl.BlockSpec((width, block), lambda at: (0, at)),
            pl.BlockSpec((owners, wide, block), moved),
        ],
        out_shape=[
            jax.ShapeDtypeStruct((1, rows), jnp.float32),
            jax.ShapeDtypeStruct((width, width_two), jnp.float32),
            jax.ShapeDtypeStruct((width_two, 1), jnp.float32),
            jax.ShapeDtypeStruct((width, rows), jnp.bfloat16),
            jax.ShapeDtypeStruct((owners, wide, rows), jnp.bfloat16),
        ],
        compiler_params=params(60),
        cost_estimate=cost(4 * depth * rows * width, 24 * depth * rows),
    )(
        mine,
        hidden,
        second,
        second.T,
        out_weight.reshape(width_two, 1),
        upstream.reshape(1, rows),
        weights,
        own,
    )


def turn_back(rows, latent, lanes, turned_ref, planes_ref):
    for k in range(latent):
        plane = turned_ref[pl.ds(k, lanes, stride=latent), :]
        planes_ref[pl.ds(k, rows, stride=latent), :] = plane.T
    return planes_ref[...].reshape(rows, latent, lanes)


def own_back_part(
    mine_ref, weights_ref, grad_hidden_ref, other_ref, back_ref, planes_ref, turned_ref
):
    rows, latent, lanes = back_ref.shape
    half = lanes // 2
    shape = (half, latent, rows)
    slot = lax.broadcasted_iota(jnp.int32, shape, 0)
    low = slot <= mine_ref[0]
    others = other_ref[...].astype(jnp.float32).reshape(half, 2, latent, rows)
    grad_hidden = grad_hidden_ref[...]
    first = jnp.dot(weights_ref[0], grad_hidden, preferred_element_type=jnp.float32)
    first = jnp.where(slot == mine_ref[0], 0.0, first.reshape(shape) * others[:, 0])
    second = jnp.dot(weights_ref[1], grad_hidden, preferred_element_type=jnp.float32)
    second = second.reshape(shape) * others[:, 1]
    turned = jnp.stack([jnp.where(low, second, first), jnp.where(low, first, second)], axis=1)
    turned_ref[...] = turned.reshape(lanes * latent, rows)
    back_ref[...] = turn_back(rows, latent, lanes, turned_ref, planes_ref)


def final_part(mine_ref, back_ref, arrived_ref, grads_ref, planes_ref, turned_ref):
    rows, latent, lanes = back_ref.shape
    turned_ref[...] = arrived_ref[...].astype(jnp.float32).reshape(lanes * latent, rows)
    arrived = turn_back(rows, latent, lanes, turned_ref, planes_ref)
    owner, parity = lane_owner((1, latent, lanes))
    kept = own_field(owner, parity, mine_ref[0])
    came = sent_field(owner, parity, mine_ref[0])
    own = back_ref[...]
    for f in range(2):
        grads_ref[:, f] = jnp.where(kept == f, own, 0.0) + jnp.where(came == f, arrived, 0.0)


def own_back_kernel(mine_ref, weights_ref, grad_hidden_ref, other_ref, back_ref, *scratch):
    for piece in pieces(back_ref.shape[0]):
        own_back_part(
            mine_ref,
            weights_ref,
            grad_hidden_ref.at[:, piece],
            other_ref.at[:, :, piece],
            back_ref.at[piece],
            *scratch,
        )


def final_kernel(mine_ref, back_ref, arrived_ref, grads_ref, *scratch):
    for piece in pieces(back_ref.shape[0]):
        final_part(
            mine_ref,
            back_ref.at[piece],
            arrived_ref.at[:, :, piece],
            grads_ref.at[piece],
            *scratch,
        )


def turn_scratch(block, latent, lanes):
    block = min(block, LANES)
    return [
        pltpu.VMEM((block * latent, lanes), jnp.float32),
        pltpu.VMEM((lanes * latent, block), jnp.float32),
    ]


def turn_own_grads(mine, weights, grad_hidden, other):
    width, rows = grad_hidden.shape
    owners, wide, _ = other.shape
    latent, lanes, block = wide // 2, 2 * owners, min(rows, TURN)
    return pl.pallas_call(
        own_back_kernel,
        grid=(rows // block,),
        in_specs=[
            SMEM_SPEC,
            pl.BlockSpec(weights.shape, lambda at: (0, 0, 0)),
            pl.BlockSpec((width, block), lambda at: (0, at)),
            pl.BlockSpec((owners, wide, block), lambda at: (0, 0, at)),
        ],
        out_specs=pl.BlockSpec((block, latent, lanes), lambda at: (at, 0, 0)),
        out_shape=jax.ShapeDtypeStruct((rows, latent, lanes), jnp.float32),
        scratch_shapes=turn_scratch(block, latent, lanes),
        compiler_params=params(60),
        cost_estimate=cost(2 * weights.size * rows, other.size * 6),
    )(mine, weights, grad_hidden, other)


def join_grads(mine, back, arrived):
    rows, latent, lanes = back.shape
    owners, wide, _ = arrived.shape
    block = min(rows, TURN)
    return pl.pallas_call(
        final_kernel,
        grid=(rows // block,),
        in_specs=[
            SMEM_SPEC,
            pl.BlockSpec((block, latent, lanes), lambda at: (at, 0, 0)),
            pl.BlockSpec((owners, wide, block), lambda at: (0, 0, at)),
        ],
        out_specs=pl.BlockSpec((block, 2, latent, lanes), lambda at: (at, 0, 0, 0)),
        out_shape=jax.ShapeDtypeStruct((rows, 2, latent, lanes), jnp.float32),
        scratch_shapes=turn_scratch(block, latent, lanes),
        compiler_params=params(60),
        cost_estimate=cost(0, back.size * 14),
    )(mine, back, arrived)


def inner_groups(owners):
    return [[base + at for at in range(PLANE)] for base in range(0, owners, PLANE)]


def outer_groups(owners):
    return [[base + at for base in range(0, owners, PLANE)] for at in range(PLANE)]


def exchange(blocks, groups=None):
    return lax.all_to_all(blocks, "field", 0, 0, axis_index_groups=groups, tiled=True)


def field_sum(partial):
    owners = lax.axis_size("field")
    inner, outer = inner_groups(owners), outer_groups(owners)
    depth = owners // PLANE
    units, rows = partial.shape
    share = exchange(partial.reshape(PLANE, units // PLANE, rows), inner)
    share = jnp.sum(share.astype(jnp.float32), axis=0)
    share = exchange(share.reshape(depth, units // owners, rows), outer)
    share = jnp.sum(share, axis=0).astype(jnp.bfloat16)
    copies = jnp.broadcast_to(share[None], (depth,) + share.shape)
    plane = exchange(copies, outer).reshape(units // PLANE, rows)
    copies = jnp.broadcast_to(plane[None], (PLANE,) + plane.shape)
    return exchange(copies, inner).reshape(units, rows)


def swap(value, pairs):
    return lax.ppermute(value, "batch", pairs)


def part_of(value, index, axis):
    return lax.dynamic_index_in_dim(value, index, axis, keepdims=False)


def core_share(value, core, axis):
    return part_of(value, core, axis) + swap(part_of(value, 1 - core, axis), CORE_PAIRS)


def per_device(vectors, first_weight, second_weight, out_weight, upstream):
    local_fields, half, latent, width = first_weight.shape
    mine = lax.axis_index("field").astype(jnp.int32).reshape(1)
    turned = jnp.transpose(vectors, (0, 1, 3, 2))
    weights = first_weight.reshape(local_fields, half * latent, width)
    other = exchange(make_send(mine, turned))
    own = make_own(mine, turned)
    pairs, partial = make_pairs(mine, own, other, jnp.transpose(weights, (0, 2, 1)))
    hidden = field_sum(partial)
    logits, grad_second, grad_out, grad_hidden, returning = run_head(
        mine, hidden, second_weight, out_weight, upstream, weights, own, latent
    )
    arrived = exchange(returning)
    place = lax.axis_index("batch")
    far, core = place // 2, place % 2
    share_first = lax.dot_general(
        pairs.reshape(-1, pairs.shape[2]), grad_hidden, NT, preferred_element_type=jnp.float32
    ).reshape(local_fields, 2, 2, half // 4, latent, width)
    share_first = core_share(share_first, core, 2)
    give_first = part_of(share_first, 1 - far, 1).astype(jnp.bfloat16)
    rows_second, width_second = grad_second.shape
    share_second = core_share(grad_second.reshape(2, rows_second // 2, width_second), core, 0)
    give_first, share_second, grad_hidden = lax.optimization_barrier(
        (give_first, share_second, grad_hidden)
    )
    take_first = swap(give_first, FAR_PAIRS)
    share_second = share_second + swap(share_second, FAR_PAIRS)
    mate_second = swap(share_second, CORE_PAIRS)
    grad_out = grad_out.reshape(-1)
    grad_out = grad_out + swap(grad_out, CORE_PAIRS)
    grad_out = grad_out + swap(grad_out, FAR_PAIRS)
    back = turn_own_grads(mine, weights, grad_hidden, other)
    grad_vectors = join_grads(mine, back, arrived)
    share_first, share_second, grad_vectors = lax.optimization_barrier(
        (share_first, share_second, grad_vectors)
    )
    grad_first = part_of(share_first, far, 1) + take_first.astype(jnp.float32)
    grad_second = jnp.stack(
        [
            jnp.where(core == 0, share_second, mate_second),
            jnp.where(core == 0, mate_second, share_second),
        ]
    ).reshape(rows_second, width_second)
    grad_vectors = jnp.transpose(grad_vectors, (0, 1, 3, 2))
    return (logits.reshape(-1), grad_vectors, grad_first, grad_second, grad_out)


def solution(mesh):
    return jax.shard_map(
        per_device,
        mesh=mesh,
        in_specs=(
            P("batch", "field", None, None),
            P("field", None, None, None),
            P(),
            P(),
            P("batch"),
        ),
        out_specs=(
            P("batch"),
            P("batch", "field", None, None),
            P("field", "batch", None, None),
            P(),
            P(),
        ),
        check_vma=False,
    )
```

```python
import jax
import jax.numpy as jnp
from jax import lax
from jax.experimental import pallas as pl
from jax.experimental.pallas import tpu as pltpu
from jax.sharding import PartitionSpec as P

PLANE = 16
LANES = 128
TURN = 512
CHUNKS = 2
MIB = 1024 * 1024
CORE_PAIRS = [(0, 1), (1, 0), (2, 3), (3, 2)]
FAR_PAIRS = [(0, 2), (2, 0), (1, 3), (3, 1)]
NT = (((1,), (1,)), ((), ()))


def silu_slope(value):
    sigmoid_value = jax.nn.sigmoid(value)
    return sigmoid_value * (1.0 + value * (1.0 - sigmoid_value))


def params(mib):
    return pltpu.CompilerParams(vmem_limit_bytes=mib * MIB)


def cost(flops, moved):
    return pl.CostEstimate(flops=flops, bytes_accessed=moved, transcendentals=0)


SMEM_SPEC = pl.BlockSpec(memory_space=pltpu.SMEM)


def lane_owner(shape):
    lane = lax.broadcasted_iota(jnp.int32, shape, len(shape) - 1)
    return lane // 2, lane % 2


def own_field(owner, parity, mine):
    return jnp.where(owner <= mine, 1 - parity, parity)


def sent_field(owner, parity, mine):
    return jnp.where(owner >= mine, 1 - parity, parity)


def turn_out(chosen, planes_ref, turned_ref):
    rows, latent, lanes = chosen.shape
    planes_ref[...] = chosen.reshape(rows * latent, lanes)
    for k in range(latent):
        plane = planes_ref[pl.ds(k, rows, stride=latent), :]
        turned_ref[pl.ds(k, lanes, stride=latent), :] = plane.T


def send_part(mine_ref, vectors_ref, send_ref, planes_ref, turned_ref):
    rows, _, latent, lanes = vectors_ref.shape
    owner, parity = lane_owner((1, latent, lanes))
    field = sent_field(owner, parity, mine_ref[0])
    chosen = jnp.where(
        field == 1, vectors_ref[:, 1].astype(jnp.float32), vectors_ref[:, 0].astype(jnp.float32)
    )
    turn_out(chosen, planes_ref, turned_ref)
    send_ref[...] = turned_ref[...].astype(jnp.bfloat16).reshape(send_ref.shape)


def own_part(mine_ref, vectors_ref, own_ref, planes_ref, turned_ref):
    rows, _, latent, lanes = vectors_ref.shape
    half = lanes // 2
    owner, parity = lane_owner((1, latent, lanes))
    field = own_field(owner, parity, mine_ref[0])
    chosen = jnp.where(
        field == 1, vectors_ref[:, 1].astype(jnp.float32), vectors_ref[:, 0].astype(jnp.float32)
    )
    turn_out(chosen, planes_ref, turned_ref)
    turned = turned_ref[...].reshape(half, 2, latent, rows)
    low = lax.broadcasted_iota(jnp.int32, (half, latent, rows), 0) <= mine_ref[0]
    even, odd = turned[:, 0], turned[:, 1]
    own_ref[0] = jnp.where(low, odd, even).astype(jnp.bfloat16).reshape(half * latent, rows)
    own_ref[1] = jnp.where(low, even, odd).astype(jnp.bfloat16).reshape(half * latent, rows)


def pieces(rows):
    return [pl.ds(at, min(rows, LANES)) for at in range(0, rows, LANES)]


def send_kernel(mine_ref, vectors_ref, send_ref, *scratch):
    for piece in pieces(vectors_ref.shape[0]):
        send_part(mine_ref, vectors_ref.at[piece], send_ref.at[:, :, piece], *scratch)


def own_kernel(mine_ref, vectors_ref, own_ref, *scratch):
    for piece in pieces(vectors_ref.shape[0]):
        own_part(mine_ref, vectors_ref.at[piece], own_ref.at[:, :, piece], *scratch)


def turn_call(kernel, mine, vectors, out_shape, out_block, out_map, block):
    rows, local_fields, latent, lanes = vectors.shape
    return pl.pallas_call(
        kernel,
        grid=(rows // block,),
        in_specs=[
            SMEM_SPEC,
            pl.BlockSpec((block, local_fields, latent, lanes), lambda at: (at, 0, 0, 0)),
        ],
        out_specs=pl.BlockSpec(out_block, out_map),
        out_shape=jax.ShapeDtypeStruct(out_shape, jnp.bfloat16),
        scratch_shapes=turn_scratch(block, latent, lanes),
        compiler_params=params(60),
        cost_estimate=cost(0, vectors.size * 3),
    )(mine, vectors)


def make_send(mine, vectors):
    rows, _, latent, lanes = vectors.shape
    owners, block = lanes // 2, min(rows, TURN)
    return turn_call(
        send_kernel,
        mine,
        vectors,
        (owners, 2 * latent, rows),
        (owners, 2 * latent, block),
        lambda at: (0, 0, at),
        block,
    )


def make_own(mine, vectors):
    rows, _, latent, lanes = vectors.shape
    half, block = lanes // 2, min(rows, TURN)
    return turn_call(
        own_kernel,
        mine,
        vectors,
        (2, half * latent, rows),
        (2, half * latent, block),
        lambda at: (0, 0, at),
        block,
    )


def products(mine_ref, own_ref, other_ref, first):
    slots, wide, rows = other_ref.shape
    latent = wide // 2
    others = other_ref[...].astype(jnp.float32).reshape(slots, 2, latent, rows)
    parts = []
    for i in range(2):
        part = own_ref[i].astype(jnp.float32).reshape(slots, latent, rows) * others[:, i]
        if i == 0:
            part = jnp.where(own_slot(mine_ref, part.shape, first), 0.0, part)
        parts.append(part.astype(jnp.bfloat16).reshape(slots * latent, rows))
    return parts


def own_slot(mine_ref, shape, first):
    return lax.broadcasted_iota(jnp.int32, shape, 0) + first == mine_ref[0]


def pairs_kernel(mine_ref, own_ref, other_ref, weights_ref, partial_ref):
    first, second = products(mine_ref, own_ref, other_ref, 0)
    total = jnp.dot(weights_ref[0], first, preferred_element_type=jnp.float32)
    total += jnp.dot(weights_ref[1], second, preferred_element_type=jnp.float32)
    partial_ref[...] = total.astype(jnp.bfloat16)


def make_partial(mine, own, other, weights_turned):
    _, depth, rows = own.shape
    owners, wide, _ = other.shape
    width = weights_turned.shape[1]
    block = min(rows, 512)
    return pl.pallas_call(
        pairs_kernel,
        grid=(rows // block,),
        in_specs=[
            SMEM_SPEC,
            pl.BlockSpec((2, depth, block), lambda at: (0, 0, at)),
            pl.BlockSpec((owners, wide, block), lambda at: (0, 0, at)),
            pl.BlockSpec((2, width, depth), lambda at: (0, 0, 0)),
        ],
        out_specs=pl.BlockSpec((width, block), lambda at: (0, at)),
        out_shape=jax.ShapeDtypeStruct((width, rows), jnp.bfloat16),
        compiler_params=params(24),
        cost_estimate=cost(4 * depth * rows * width, 16 * depth * rows),
    )(mine, own, other, weights_turned)


def grad_first_kernel(mine_ref, own_ref, other_ref, grad_hidden_ref, grads_ref):
    first = pl.program_id(0) * other_ref.shape[0]
    for i, pairs in enumerate(products(mine_ref, own_ref, other_ref, first)):
        grads_ref[i] = lax.dot_general(
            pairs, grad_hidden_ref[...], NT, preferred_element_type=jnp.float32
        )


def make_grad_first(mine, own, other, grad_hidden):
    _, depth, rows = own.shape
    owners, wide, _ = other.shape
    width = grad_hidden.shape[0]
    return pl.pallas_call(
        grad_first_kernel,
        grid=(CHUNKS,),
        in_specs=[
            SMEM_SPEC,
            pl.BlockSpec((2, depth // CHUNKS, rows), lambda at: (0, at, 0)),
            pl.BlockSpec((owners // CHUNKS, wide, rows), lambda at: (at, 0, 0)),
            pl.BlockSpec((width, rows), lambda at: (0, 0)),
        ],
        out_specs=pl.BlockSpec((2, depth // CHUNKS, width), lambda at: (0, at, 0)),
        out_shape=jax.ShapeDtypeStruct((2, depth, width), jnp.float32),
        compiler_params=params(60),
        cost_estimate=cost(4 * depth * rows * width, 16 * depth * rows),
    )(mine, own, other, grad_hidden)


def head_kernel(
    mine_ref,
    hidden_ref,
    second_ref,
    second_turned_ref,
    out_weight_ref,
    upstream_ref,
    weights_ref,
    own_ref,
    logits_ref,
    grad_second_ref,
    grad_out_ref,
    grad_hidden_ref,
    returning_ref,
):
    slots, wide, rows = returning_ref.shape
    latent = wide // 2

    @pl.when(pl.program_id(0) == 0)
    def _():
        hidden = hidden_ref[...].astype(jnp.float32)
        sigmoid_hidden = jax.nn.sigmoid(hidden)
        activated = (hidden * sigmoid_hidden).astype(jnp.bfloat16)
        second_pre = jnp.dot(second_turned_ref[...], activated, preferred_element_type=jnp.float32)
        sigmoid_pre = jax.nn.sigmoid(second_pre)
        second_act = second_pre * sigmoid_pre
        out_weight = out_weight_ref[...]
        upstream = upstream_ref[...]
        logits_ref[...] = jnp.sum(second_act * out_weight, axis=0, keepdims=True)
        slope = sigmoid_pre * (1.0 + second_pre * (1.0 - sigmoid_pre))
        grad_pre = (upstream * out_weight * slope).astype(jnp.bfloat16)
        grad_second_ref[...] = lax.dot_general(
            activated, grad_pre, NT, preferred_element_type=jnp.float32
        )
        grad_out_ref[...] = jnp.sum(second_act * upstream, axis=1, keepdims=True)
        back_hidden = jnp.dot(second_ref[...], grad_pre, preferred_element_type=jnp.float32)
        slope = sigmoid_hidden * (1.0 + hidden * (1.0 - sigmoid_hidden))
        grad_hidden_ref[...] = (back_hidden * slope).astype(jnp.bfloat16)

    first = pl.program_id(0) * slots
    returning = []
    for i in range(2):
        grads = jnp.dot(weights_ref[i], grad_hidden_ref[...], preferred_element_type=jnp.float32)
        grads = grads.reshape(slots, latent, rows)
        if i == 0:
            grads = jnp.where(own_slot(mine_ref, grads.shape, first), 0.0, grads)
        own = own_ref[i].astype(jnp.float32).reshape(slots, latent, rows)
        returning.append(grads * own)
    returning = jnp.stack(returning, axis=1).reshape(returning_ref.shape)
    returning_ref[...] = returning.astype(jnp.bfloat16)


def run_head(mine, hidden, second, out_weight, upstream, weights, own, latent):
    width, rows = hidden.shape
    _, depth, _ = own.shape
    owners, wide = depth // latent, 2 * latent
    width_two = second.shape[1]
    fixed = lambda at: (0, 0)
    return pl.pallas_call(
        head_kernel,
        grid=(CHUNKS,),
        in_specs=[
            SMEM_SPEC,
            pl.BlockSpec((width, rows), fixed),
            pl.BlockSpec((width, width_two), fixed),
            pl.BlockSpec((width_two, width), fixed),
            pl.BlockSpec((width_two, 1), fixed),
            pl.BlockSpec((1, rows), fixed),
            pl.BlockSpec((2, depth // CHUNKS, width), lambda at: (0, at, 0)),
            pl.BlockSpec((2, depth // CHUNKS, rows), lambda at: (0, at, 0)),
        ],
        out_specs=[
            pl.BlockSpec((1, rows), fixed),
            pl.BlockSpec((width, width_two), fixed),
            pl.BlockSpec((width_two, 1), fixed),
            pl.BlockSpec((width, rows), fixed),
            pl.BlockSpec((owners // CHUNKS, wide, rows), lambda at: (at, 0, 0)),
        ],
        out_shape=[
            jax.ShapeDtypeStruct((1, rows), jnp.float32),
            jax.ShapeDtypeStruct((width, width_two), jnp.float32),
            jax.ShapeDtypeStruct((width_two, 1), jnp.float32),
            jax.ShapeDtypeStruct((width, rows), jnp.bfloat16),
            jax.ShapeDtypeStruct((owners, wide, rows), jnp.bfloat16),
        ],
        compiler_params=params(60),
        cost_estimate=cost(4 * depth * rows * width, 24 * depth * rows),
    )(
        mine,
        hidden,
        second,
        second.T,
        out_weight.reshape(width_two, 1),
        upstream.reshape(1, rows),
        weights,
        own,
    )


def turn_back(rows, latent, lanes, turned_ref, planes_ref):
    for k in range(latent):
        plane = turned_ref[pl.ds(k, lanes, stride=latent), :]
        planes_ref[pl.ds(k, rows, stride=latent), :] = plane.T
    return planes_ref[...].reshape(rows, latent, lanes)


def own_back_part(
    mine_ref, weights_ref, grad_hidden_ref, other_ref, back_ref, planes_ref, turned_ref
):
    rows, latent, lanes = back_ref.shape
    half = lanes // 2
    shape = (half, latent, rows)
    slot = lax.broadcasted_iota(jnp.int32, shape, 0)
    low = slot <= mine_ref[0]
    others = other_ref[...].astype(jnp.float32).reshape(half, 2, latent, rows)
    grad_hidden = grad_hidden_ref[...]
    first = jnp.dot(weights_ref[0], grad_hidden, preferred_element_type=jnp.float32)
    first = jnp.where(slot == mine_ref[0], 0.0, first.reshape(shape) * others[:, 0])
    second = jnp.dot(weights_ref[1], grad_hidden, preferred_element_type=jnp.float32)
    second = second.reshape(shape) * others[:, 1]
    turned = jnp.stack([jnp.where(low, second, first), jnp.where(low, first, second)], axis=1)
    turned_ref[...] = turned.reshape(lanes * latent, rows)
    back_ref[...] = turn_back(rows, latent, lanes, turned_ref, planes_ref)


def final_part(mine_ref, back_ref, arrived_ref, grads_ref, planes_ref, turned_ref):
    rows, latent, lanes = back_ref.shape
    turned_ref[...] = arrived_ref[...].astype(jnp.float32).reshape(lanes * latent, rows)
    arrived = turn_back(rows, latent, lanes, turned_ref, planes_ref)
    owner, parity = lane_owner((1, latent, lanes))
    kept = own_field(owner, parity, mine_ref[0])
    came = sent_field(owner, parity, mine_ref[0])
    own = back_ref[...]
    for f in range(2):
        grads_ref[:, f] = jnp.where(kept == f, own, 0.0) + jnp.where(came == f, arrived, 0.0)


def own_back_kernel(mine_ref, weights_ref, grad_hidden_ref, other_ref, back_ref, *scratch):
    for piece in pieces(back_ref.shape[0]):
        own_back_part(
            mine_ref,
            weights_ref,
            grad_hidden_ref.at[:, piece],
            other_ref.at[:, :, piece],
            back_ref.at[piece],
            *scratch,
        )


def final_kernel(mine_ref, back_ref, arrived_ref, grads_ref, *scratch):
    for piece in pieces(back_ref.shape[0]):
        final_part(
            mine_ref,
            back_ref.at[piece],
            arrived_ref.at[:, :, piece],
            grads_ref.at[piece],
            *scratch,
        )


def turn_scratch(block, latent, lanes):
    block = min(block, LANES)
    return [
        pltpu.VMEM((block * latent, lanes), jnp.float32),
        pltpu.VMEM((lanes * latent, block), jnp.float32),
    ]


def turn_own_grads(mine, weights, grad_hidden, other):
    width, rows = grad_hidden.shape
    owners, wide, _ = other.shape
    latent, lanes, block = wide // 2, 2 * owners, min(rows, TURN)
    return pl.pallas_call(
        own_back_kernel,
        grid=(rows // block,),
        in_specs=[
            SMEM_SPEC,
            pl.BlockSpec(weights.shape, lambda at: (0, 0, 0)),
            pl.BlockSpec((width, block), lambda at: (0, at)),
            pl.BlockSpec((owners, wide, block), lambda at: (0, 0, at)),
        ],
        out_specs=pl.BlockSpec((block, latent, lanes), lambda at: (at, 0, 0)),
        out_shape=jax.ShapeDtypeStruct((rows, latent, lanes), jnp.float32),
        scratch_shapes=turn_scratch(block, latent, lanes),
        compiler_params=params(60),
        cost_estimate=cost(2 * weights.size * rows, other.size * 6),
    )(mine, weights, grad_hidden, other)


def join_grads(mine, back, arrived):
    rows, latent, lanes = back.shape
    owners, wide, _ = arrived.shape
    block = min(rows, TURN)
    return pl.pallas_call(
        final_kernel,
        grid=(rows // block,),
        in_specs=[
            SMEM_SPEC,
            pl.BlockSpec((block, latent, lanes), lambda at: (at, 0, 0)),
            pl.BlockSpec((owners, wide, block), lambda at: (0, 0, at)),
        ],
        out_specs=pl.BlockSpec((block, 2, latent, lanes), lambda at: (at, 0, 0, 0)),
        out_shape=jax.ShapeDtypeStruct((rows, 2, latent, lanes), jnp.float32),
        scratch_shapes=turn_scratch(block, latent, lanes),
        compiler_params=params(48),
        cost_estimate=cost(0, back.size * 14),
    )(mine, back, arrived)


def inner_groups(owners):
    return [[base + at for at in range(PLANE)] for base in range(0, owners, PLANE)]


def outer_groups(owners):
    return [[base + at for base in range(0, owners, PLANE)] for at in range(PLANE)]


def exchange(blocks, groups=None):
    return lax.all_to_all(blocks, "field", 0, 0, axis_index_groups=groups, tiled=True)


def field_sum(partial):
    owners = lax.axis_size("field")
    inner, outer = inner_groups(owners), outer_groups(owners)
    depth = owners // PLANE
    units, rows = partial.shape
    share = exchange(partial.reshape(PLANE, units // PLANE, rows), inner)
    share = jnp.sum(share.astype(jnp.float32), axis=0).astype(jnp.bfloat16)
    copies = jnp.broadcast_to(share[None], (depth,) + share.shape)
    share = jnp.sum(exchange(copies, outer).astype(jnp.float32), axis=0).astype(jnp.bfloat16)
    copies = jnp.broadcast_to(share[None], (PLANE,) + share.shape)
    return exchange(copies, inner).reshape(units, rows)


def swap(value, pairs):
    return lax.ppermute(value, "batch", pairs)


def part_of(value, index, axis):
    return lax.dynamic_index_in_dim(value, index, axis, keepdims=False)


def core_share(value, core, axis):
    return part_of(value, core, axis) + swap(part_of(value, 1 - core, axis), CORE_PAIRS)


def per_device(vectors, first_weight, second_weight, out_weight, upstream):
    local_fields, half, latent, width = first_weight.shape
    mine = lax.axis_index("field").astype(jnp.int32).reshape(1)
    turned = jnp.transpose(vectors, (0, 1, 3, 2))
    weights = first_weight.reshape(local_fields, half * latent, width)
    other = exchange(make_send(mine, turned))
    own = make_own(mine, turned)
    partial = make_partial(mine, own, other, jnp.transpose(weights, (0, 2, 1)))
    hidden = field_sum(partial)
    logits, grad_second, grad_out, grad_hidden, returning = run_head(
        mine, hidden, second_weight, out_weight, upstream, weights, own, latent
    )
    arrived = exchange(returning)
    place = lax.axis_index("batch")
    far, core = place // 2, place % 2
    share_first = make_grad_first(mine, own, other, grad_hidden)
    share_first = share_first.reshape(local_fields, 2, 2, half // 4, latent, width)
    share_first = core_share(share_first, core, 2)
    give_first = part_of(share_first, 1 - far, 1).astype(jnp.bfloat16)
    rows_second, width_second = grad_second.shape
    share_second = core_share(grad_second.reshape(2, rows_second // 2, width_second), core, 0)
    give_first, share_second, grad_hidden = lax.optimization_barrier(
        (give_first, share_second, grad_hidden)
    )
    take_first = swap(give_first, FAR_PAIRS)
    take_second = swap(share_second, FAR_PAIRS)
    grad_out = grad_out.reshape(-1)
    grad_out = grad_out + swap(grad_out, CORE_PAIRS)
    take_out = swap(grad_out, FAR_PAIRS)
    back = turn_own_grads(mine, weights, grad_hidden, other)
    share_first, share_second, grad_out, back = lax.optimization_barrier(
        (share_first, share_second, grad_out, back)
    )
    grad_out = grad_out + take_out
    share_second = share_second + take_second
    mate_second = swap(share_second, CORE_PAIRS)
    grad_vectors = join_grads(mine, back, arrived)
    grad_first = part_of(share_first, far, 1) + take_first.astype(jnp.float32)
    grad_second = jnp.stack(
        [
            jnp.where(core == 0, share_second, mate_second),
            jnp.where(core == 0, mate_second, share_second),
        ]
    ).reshape(rows_second, width_second)
    grad_vectors = jnp.transpose(grad_vectors, (0, 1, 3, 2))
    return (logits.reshape(-1), grad_vectors, grad_first, grad_second, grad_out)


def solution(mesh):
    return jax.shard_map(
        per_device,
        mesh=mesh,
        in_specs=(
            P("batch", "field", None, None),
            P("field", None, None, None),
            P(),
            P(),
            P("batch"),
        ),
        out_specs=(
            P("batch"),
            P("batch", "field", None, None),
            P("field", "batch", None, None),
            P(),
            P(),
        ),
        check_vma=False,
    )
```

```python
import jax
import jax.numpy as jnp
from jax import lax
from jax.experimental import pallas as pl
from jax.experimental.pallas import tpu as pltpu
from jax.sharding import PartitionSpec as P

PLANE = 16
LANES = 128
TURN = 512
CHUNKS = 2
MIB = 1024 * 1024
CORE_PAIRS = [(0, 1), (1, 0), (2, 3), (3, 2)]
FAR_PAIRS = [(0, 2), (2, 0), (1, 3), (3, 1)]
NT = (((1,), (1,)), ((), ()))


def silu_slope(value):
    sigmoid_value = jax.nn.sigmoid(value)
    return sigmoid_value * (1.0 + value * (1.0 - sigmoid_value))


def params(mib):
    return pltpu.CompilerParams(vmem_limit_bytes=mib * MIB)


def cost(flops, moved):
    return pl.CostEstimate(flops=flops, bytes_accessed=moved, transcendentals=0)


SMEM_SPEC = pl.BlockSpec(memory_space=pltpu.SMEM)


def lane_owner(shape):
    lane = lax.broadcasted_iota(jnp.int32, shape, len(shape) - 1)
    return lane // 2, lane % 2


def own_field(owner, parity, mine):
    return jnp.where(owner <= mine, 1 - parity, parity)


def sent_field(owner, parity, mine):
    return jnp.where(owner >= mine, 1 - parity, parity)


def turn_out(chosen, planes_ref, turned_ref):
    rows, latent, lanes = chosen.shape
    planes_ref[...] = chosen.reshape(rows * latent, lanes)
    for k in range(latent):
        plane = planes_ref[pl.ds(k, rows, stride=latent), :]
        turned_ref[pl.ds(k, lanes, stride=latent), :] = plane.T


def send_part(mine_ref, vectors_ref, send_ref, planes_ref, turned_ref):
    rows, _, latent, lanes = vectors_ref.shape
    owner, parity = lane_owner((1, latent, lanes))
    field = sent_field(owner, parity, mine_ref[0])
    chosen = jnp.where(
        field == 1, vectors_ref[:, 1].astype(jnp.float32), vectors_ref[:, 0].astype(jnp.float32)
    )
    turn_out(chosen, planes_ref, turned_ref)
    send_ref[...] = turned_ref[...].astype(jnp.bfloat16).reshape(send_ref.shape)


def own_part(mine_ref, vectors_ref, own_ref, planes_ref, turned_ref):
    rows, _, latent, lanes = vectors_ref.shape
    half = lanes // 2
    owner, parity = lane_owner((1, latent, lanes))
    field = own_field(owner, parity, mine_ref[0])
    chosen = jnp.where(
        field == 1, vectors_ref[:, 1].astype(jnp.float32), vectors_ref[:, 0].astype(jnp.float32)
    )
    turn_out(chosen, planes_ref, turned_ref)
    turned = turned_ref[...].reshape(half, 2, latent, rows)
    low = lax.broadcasted_iota(jnp.int32, (half, latent, rows), 0) <= mine_ref[0]
    even, odd = turned[:, 0], turned[:, 1]
    own_ref[0] = jnp.where(low, odd, even).astype(jnp.bfloat16).reshape(half * latent, rows)
    own_ref[1] = jnp.where(low, even, odd).astype(jnp.bfloat16).reshape(half * latent, rows)


def pieces(rows):
    return [pl.ds(at, min(rows, LANES)) for at in range(0, rows, LANES)]


def send_kernel(mine_ref, vectors_ref, send_ref, *scratch):
    for piece in pieces(vectors_ref.shape[0]):
        send_part(mine_ref, vectors_ref.at[piece], send_ref.at[:, :, piece], *scratch)


def own_kernel(mine_ref, vectors_ref, own_ref, *scratch):
    for piece in pieces(vectors_ref.shape[0]):
        own_part(mine_ref, vectors_ref.at[piece], own_ref.at[:, :, piece], *scratch)


def turn_call(kernel, mine, vectors, out_shape, out_block, out_map, block):
    rows, local_fields, latent, lanes = vectors.shape
    return pl.pallas_call(
        kernel,
        grid=(rows // block,),
        in_specs=[
            SMEM_SPEC,
            pl.BlockSpec((block, local_fields, latent, lanes), lambda at: (at, 0, 0, 0)),
        ],
        out_specs=pl.BlockSpec(out_block, out_map),
        out_shape=jax.ShapeDtypeStruct(out_shape, jnp.bfloat16),
        scratch_shapes=turn_scratch(block, latent, lanes),
        compiler_params=params(60),
        cost_estimate=cost(0, vectors.size * 3),
    )(mine, vectors)


def make_send(mine, vectors):
    rows, _, latent, lanes = vectors.shape
    owners, block = lanes // 2, min(rows, TURN)
    return turn_call(
        send_kernel,
        mine,
        vectors,
        (owners, 2 * latent, rows),
        (owners, 2 * latent, block),
        lambda at: (0, 0, at),
        block,
    )


def make_own(mine, vectors):
    rows, _, latent, lanes = vectors.shape
    half, block = lanes // 2, min(rows, TURN)
    return turn_call(
        own_kernel,
        mine,
        vectors,
        (2, half * latent, rows),
        (2, half * latent, block),
        lambda at: (0, 0, at),
        block,
    )


def products(mine_ref, own_ref, other_ref, first):
    slots, wide, rows = other_ref.shape
    latent = wide // 2
    others = other_ref[...].astype(jnp.float32).reshape(slots, 2, latent, rows)
    parts = []
    for i in range(2):
        part = own_ref[i].astype(jnp.float32).reshape(slots, latent, rows) * others[:, i]
        if i == 0:
            part = jnp.where(own_slot(mine_ref, part.shape, first), 0.0, part)
        parts.append(part.astype(jnp.bfloat16).reshape(slots * latent, rows))
    return parts


def own_slot(mine_ref, shape, first):
    return lax.broadcasted_iota(jnp.int32, shape, 0) + first == mine_ref[0]


def pairs_kernel(mine_ref, own_ref, other_ref, weights_ref, partial_ref):
    first, second = products(mine_ref, own_ref, other_ref, 0)
    total = jnp.dot(weights_ref[0], first, preferred_element_type=jnp.float32)
    total += jnp.dot(weights_ref[1], second, preferred_element_type=jnp.float32)
    partial_ref[...] = total.astype(jnp.bfloat16)


def make_partial(mine, own, other, weights_turned):
    _, depth, rows = own.shape
    owners, wide, _ = other.shape
    width = weights_turned.shape[1]
    block = min(rows, 512)
    return pl.pallas_call(
        pairs_kernel,
        grid=(rows // block,),
        in_specs=[
            SMEM_SPEC,
            pl.BlockSpec((2, depth, block), lambda at: (0, 0, at)),
            pl.BlockSpec((owners, wide, block), lambda at: (0, 0, at)),
            pl.BlockSpec((2, width, depth), lambda at: (0, 0, 0)),
        ],
        out_specs=pl.BlockSpec((width, block), lambda at: (0, at)),
        out_shape=jax.ShapeDtypeStruct((width, rows), jnp.bfloat16),
        compiler_params=params(24),
        cost_estimate=cost(4 * depth * rows * width, 16 * depth * rows),
    )(mine, own, other, weights_turned)


def grad_first_kernel(mine_ref, own_ref, other_ref, grad_hidden_ref, grads_ref):
    first = pl.program_id(0) * other_ref.shape[0]
    for i, pairs in enumerate(products(mine_ref, own_ref, other_ref, first)):
        grads_ref[i] = lax.dot_general(
            pairs, grad_hidden_ref[...], NT, preferred_element_type=jnp.float32
        )


def make_grad_first(mine, own, other, grad_hidden):
    _, depth, rows = own.shape
    owners, wide, _ = other.shape
    width = grad_hidden.shape[0]
    return pl.pallas_call(
        grad_first_kernel,
        grid=(CHUNKS,),
        in_specs=[
            SMEM_SPEC,
            pl.BlockSpec((2, depth // CHUNKS, rows), lambda at: (0, at, 0)),
            pl.BlockSpec((owners // CHUNKS, wide, rows), lambda at: (at, 0, 0)),
            pl.BlockSpec((width, rows), lambda at: (0, 0)),
        ],
        out_specs=pl.BlockSpec((2, depth // CHUNKS, width), lambda at: (0, at, 0)),
        out_shape=jax.ShapeDtypeStruct((2, depth, width), jnp.float32),
        compiler_params=params(60),
        cost_estimate=cost(4 * depth * rows * width, 16 * depth * rows),
    )(mine, own, other, grad_hidden)


def head_kernel(
    mine_ref,
    hidden_ref,
    second_ref,
    second_turned_ref,
    out_weight_ref,
    upstream_ref,
    weights_ref,
    own_ref,
    logits_ref,
    grad_second_ref,
    grad_out_ref,
    grad_hidden_ref,
    returning_ref,
):
    slots, wide, rows = returning_ref.shape
    latent = wide // 2

    @pl.when(pl.program_id(0) == 0)
    def _():
        hidden = hidden_ref[...].astype(jnp.float32)
        sigmoid_hidden = jax.nn.sigmoid(hidden)
        activated = (hidden * sigmoid_hidden).astype(jnp.bfloat16)
        second_pre = jnp.dot(second_turned_ref[...], activated, preferred_element_type=jnp.float32)
        sigmoid_pre = jax.nn.sigmoid(second_pre)
        second_act = second_pre * sigmoid_pre
        out_weight = out_weight_ref[:, :1]
        upstream = upstream_ref[...]
        logits_ref[...] = jnp.sum(second_act * out_weight, axis=0, keepdims=True)
        slope = sigmoid_pre * (1.0 + second_pre * (1.0 - sigmoid_pre))
        grad_pre = (upstream * out_weight * slope).astype(jnp.bfloat16)
        grad_second_ref[...] = lax.dot_general(
            activated, grad_pre, NT, preferred_element_type=jnp.float32
        )
        grad_out_ref[...] = jnp.sum(second_act * upstream, axis=1, keepdims=True)
        back_hidden = jnp.dot(second_ref[...], grad_pre, preferred_element_type=jnp.float32)
        slope = sigmoid_hidden * (1.0 + hidden * (1.0 - sigmoid_hidden))
        grad_hidden_ref[...] = (back_hidden * slope).astype(jnp.bfloat16)

    first = pl.program_id(0) * slots
    returning = []
    for i in range(2):
        grads = jnp.dot(weights_ref[i], grad_hidden_ref[...], preferred_element_type=jnp.float32)
        grads = grads.reshape(slots, latent, rows)
        if i == 0:
            grads = jnp.where(own_slot(mine_ref, grads.shape, first), 0.0, grads)
        own = own_ref[i].astype(jnp.float32).reshape(slots, latent, rows)
        returning.append(grads * own)
    returning = jnp.stack(returning, axis=1).reshape(returning_ref.shape)
    returning_ref[...] = returning.astype(jnp.bfloat16)


def run_head(
    mine, hidden, second, second_turned, out_columns, upstream, weights, own, latent
):
    width, rows = hidden.shape
    _, depth, _ = own.shape
    owners, wide = depth // latent, 2 * latent
    width_two = second.shape[1]
    fixed = lambda at: (0, 0)
    return pl.pallas_call(
        head_kernel,
        grid=(CHUNKS,),
        in_specs=[
            SMEM_SPEC,
            pl.BlockSpec((width, rows), fixed),
            pl.BlockSpec((width, width_two), fixed),
            pl.BlockSpec((width_two, width), fixed),
            pl.BlockSpec((width_two, LANES), fixed),
            pl.BlockSpec((1, rows), fixed),
            pl.BlockSpec((2, depth // CHUNKS, width), lambda at: (0, at, 0)),
            pl.BlockSpec((2, depth // CHUNKS, rows), lambda at: (0, at, 0)),
        ],
        out_specs=[
            pl.BlockSpec((1, rows), fixed),
            pl.BlockSpec((width, width_two), fixed),
            pl.BlockSpec((width_two, 1), fixed),
            pl.BlockSpec((width, rows), fixed),
            pl.BlockSpec((owners // CHUNKS, wide, rows), lambda at: (at, 0, 0)),
        ],
        out_shape=[
            jax.ShapeDtypeStruct((1, rows), jnp.float32),
            jax.ShapeDtypeStruct((width, width_two), jnp.float32),
            jax.ShapeDtypeStruct((width_two, 1), jnp.float32),
            jax.ShapeDtypeStruct((width, rows), jnp.bfloat16),
            jax.ShapeDtypeStruct((owners, wide, rows), jnp.bfloat16),
        ],
        compiler_params=params(60),
        cost_estimate=cost(4 * depth * rows * width, 24 * depth * rows),
    )(
        mine,
        hidden,
        second,
        second_turned,
        out_columns,
        upstream.reshape(1, rows),
        weights,
        own,
    )


def turn_back(rows, latent, lanes, turned_ref, planes_ref):
    for k in range(latent):
        plane = turned_ref[pl.ds(k, lanes, stride=latent), :]
        planes_ref[pl.ds(k, rows, stride=latent), :] = plane.T
    return planes_ref[...].reshape(rows, latent, lanes)


def own_back_part(
    mine_ref, weights_ref, grad_hidden_ref, other_ref, back_ref, planes_ref, turned_ref
):
    rows, latent, lanes = back_ref.shape
    half = lanes // 2
    shape = (half, latent, rows)
    slot = lax.broadcasted_iota(jnp.int32, shape, 0)
    low = slot <= mine_ref[0]
    others = other_ref[...].astype(jnp.float32).reshape(half, 2, latent, rows)
    grad_hidden = grad_hidden_ref[...]
    first = jnp.dot(weights_ref[0], grad_hidden, preferred_element_type=jnp.float32)
    first = jnp.where(slot == mine_ref[0], 0.0, first.reshape(shape) * others[:, 0])
    second = jnp.dot(weights_ref[1], grad_hidden, preferred_element_type=jnp.float32)
    second = second.reshape(shape) * others[:, 1]
    turned = jnp.stack([jnp.where(low, second, first), jnp.where(low, first, second)], axis=1)
    turned_ref[...] = turned.reshape(lanes * latent, rows)
    back_ref[...] = turn_back(rows, latent, lanes, turned_ref, planes_ref)


def final_part(mine_ref, back_ref, arrived_ref, grads_ref, planes_ref, turned_ref):
    rows, latent, lanes = back_ref.shape
    turned_ref[...] = arrived_ref[...].astype(jnp.float32).reshape(lanes * latent, rows)
    arrived = turn_back(rows, latent, lanes, turned_ref, planes_ref)
    owner, parity = lane_owner((1, latent, lanes))
    kept = own_field(owner, parity, mine_ref[0])
    came = sent_field(owner, parity, mine_ref[0])
    own = back_ref[...]
    for f in range(2):
        grads_ref[:, f] = jnp.where(kept == f, own, 0.0) + jnp.where(came == f, arrived, 0.0)


def own_back_kernel(mine_ref, weights_ref, grad_hidden_ref, other_ref, back_ref, *scratch):
    for piece in pieces(back_ref.shape[0]):
        own_back_part(
            mine_ref,
            weights_ref,
            grad_hidden_ref.at[:, piece],
            other_ref.at[:, :, piece],
            back_ref.at[piece],
            *scratch,
        )


def final_kernel(mine_ref, back_ref, arrived_ref, grads_ref, *scratch):
    for piece in pieces(back_ref.shape[0]):
        final_part(
            mine_ref,
            back_ref.at[piece],
            arrived_ref.at[:, :, piece],
            grads_ref.at[piece],
            *scratch,
        )


def turn_scratch(block, latent, lanes):
    block = min(block, LANES)
    return [
        pltpu.VMEM((block * latent, lanes), jnp.float32),
        pltpu.VMEM((lanes * latent, block), jnp.float32),
    ]


def turn_own_grads(mine, weights, grad_hidden, other):
    width, rows = grad_hidden.shape
    owners, wide, _ = other.shape
    latent, lanes, block = wide // 2, 2 * owners, min(rows, TURN)
    return pl.pallas_call(
        own_back_kernel,
        grid=(rows // block,),
        in_specs=[
            SMEM_SPEC,
            pl.BlockSpec(weights.shape, lambda at: (0, 0, 0)),
            pl.BlockSpec((width, block), lambda at: (0, at)),
            pl.BlockSpec((owners, wide, block), lambda at: (0, 0, at)),
        ],
        out_specs=pl.BlockSpec((block, latent, lanes), lambda at: (at, 0, 0)),
        out_shape=jax.ShapeDtypeStruct((rows, latent, lanes), jnp.float32),
        scratch_shapes=turn_scratch(block, latent, lanes),
        compiler_params=params(60),
        cost_estimate=cost(2 * weights.size * rows, other.size * 6),
    )(mine, weights, grad_hidden, other)


def join_grads(mine, back, arrived):
    rows, latent, lanes = back.shape
    owners, wide, _ = arrived.shape
    block = min(rows, TURN)
    return pl.pallas_call(
        final_kernel,
        grid=(rows // block,),
        in_specs=[
            SMEM_SPEC,
            pl.BlockSpec((block, latent, lanes), lambda at: (at, 0, 0)),
            pl.BlockSpec((owners, wide, block), lambda at: (0, 0, at)),
        ],
        out_specs=pl.BlockSpec((block, 2, latent, lanes), lambda at: (at, 0, 0, 0)),
        out_shape=jax.ShapeDtypeStruct((rows, 2, latent, lanes), jnp.float32),
        scratch_shapes=turn_scratch(block, latent, lanes),
        compiler_params=params(48),
        cost_estimate=cost(0, back.size * 14),
    )(mine, back, arrived)


def inner_groups(owners):
    return [[base + at for at in range(PLANE)] for base in range(0, owners, PLANE)]


def outer_groups(owners):
    return [[base + at for base in range(0, owners, PLANE)] for at in range(PLANE)]


def exchange(blocks, groups=None):
    return lax.all_to_all(blocks, "field", 0, 0, axis_index_groups=groups, tiled=True)


def field_sum(partial):
    owners = lax.axis_size("field")
    inner, outer = inner_groups(owners), outer_groups(owners)
    depth = owners // PLANE
    units, rows = partial.shape
    share = exchange(partial.reshape(PLANE, units // PLANE, rows), inner)
    share = jnp.sum(share.astype(jnp.float32), axis=0).astype(jnp.bfloat16)
    copies = jnp.broadcast_to(share[None], (depth,) + share.shape)
    share = jnp.sum(exchange(copies, outer).astype(jnp.float32), axis=0).astype(jnp.bfloat16)
    copies = jnp.broadcast_to(share[None], (PLANE,) + share.shape)
    return exchange(copies, inner).reshape(units, rows)


def swap(value, pairs):
    return lax.ppermute(value, "batch", pairs)


def part_of(value, index, axis):
    return lax.dynamic_index_in_dim(value, index, axis, keepdims=False)


def core_share(value, core, axis):
    return part_of(value, core, axis) + swap(part_of(value, 1 - core, axis), CORE_PAIRS)


def per_device(vectors, first_weight, second_weight, out_weight, upstream):
    local_fields, half, latent, width = first_weight.shape
    mine = lax.axis_index("field").astype(jnp.int32).reshape(1)
    turned = jnp.transpose(vectors, (0, 1, 3, 2))
    weights = first_weight.reshape(local_fields, half * latent, width)
    other = exchange(make_send(mine, turned))
    out_columns = jnp.broadcast_to(out_weight[:, None], (out_weight.shape[0], LANES))
    own, second_turned, out_columns = lax.optimization_barrier(
        (make_own(mine, turned), second_weight.T, out_columns)
    )
    partial = make_partial(mine, own, other, jnp.transpose(weights, (0, 2, 1)))
    hidden = field_sum(partial)
    logits, grad_second, grad_out, grad_hidden, returning = run_head(
        mine,
        hidden,
        second_weight,
        second_turned,
        out_columns,
        upstream,
        weights,
        own,
        latent,
    )
    arrived = exchange(returning)
    place = lax.axis_index("batch")
    far, core = place // 2, place % 2
    share_first = make_grad_first(mine, own, other, grad_hidden)
    share_first = share_first.reshape(local_fields, 2, 2, half // 4, latent, width)
    share_first = core_share(share_first, core, 2)
    give_first = part_of(share_first, 1 - far, 1).astype(jnp.bfloat16)
    rows_second, width_second = grad_second.shape
    share_second = core_share(grad_second.reshape(2, rows_second // 2, width_second), core, 0)
    give_first, share_second, grad_hidden = lax.optimization_barrier(
        (give_first, share_second, grad_hidden)
    )
    take_first = swap(give_first, FAR_PAIRS)
    take_second = swap(share_second, FAR_PAIRS)
    grad_out = grad_out.reshape(-1)
    grad_out = grad_out + swap(grad_out, CORE_PAIRS)
    take_out = swap(grad_out, FAR_PAIRS)
    back = turn_own_grads(mine, weights, grad_hidden, other)
    share_first, share_second, grad_out, back = lax.optimization_barrier(
        (share_first, share_second, grad_out, back)
    )
    grad_out = grad_out + take_out
    share_second = share_second + take_second
    mate_second = swap(share_second, CORE_PAIRS)
    grad_vectors = join_grads(mine, back, arrived)
    grad_first = part_of(share_first, far, 1) + take_first.astype(jnp.float32)
    grad_second = jnp.stack(
        [
            jnp.where(core == 0, share_second, mate_second),
            jnp.where(core == 0, mate_second, share_second),
        ]
    ).reshape(rows_second, width_second)
    grad_vectors = jnp.transpose(grad_vectors, (0, 1, 3, 2))
    return (logits.reshape(-1), grad_vectors, grad_first, grad_second, grad_out)


def solution(mesh):
    return jax.shard_map(
        per_device,
        mesh=mesh,
        in_specs=(
            P("batch", "field", None, None),
            P("field", None, None, None),
            P(),
            P(),
            P("batch"),
        ),
        out_specs=(
            P("batch"),
            P("batch", "field", None, None),
            P("field", "batch", None, None),
            P(),
            P(),
        ),
        check_vma=False,
    )
```

```python
import jax
import jax.numpy as jnp
from jax import lax
from jax.experimental import pallas as pl
from jax.experimental.pallas import tpu as pltpu
from jax.sharding import PartitionSpec as P

PLANE = 16
LANES = 128
TURN = 512
CHUNKS = 2
STORE = 256
MIB = 1024 * 1024
CORE_PAIRS = [(0, 1), (1, 0), (2, 3), (3, 2)]
FAR_PAIRS = [(0, 2), (2, 0), (1, 3), (3, 1)]
NT = (((1,), (1,)), ((), ()))


def silu_slope(value):
    sigmoid_value = jax.nn.sigmoid(value)
    return sigmoid_value * (1.0 + value * (1.0 - sigmoid_value))


def params(mib):
    return pltpu.CompilerParams(vmem_limit_bytes=mib * MIB)


def cost(flops, moved):
    return pl.CostEstimate(flops=flops, bytes_accessed=moved, transcendentals=0)


SMEM_SPEC = pl.BlockSpec(memory_space=pltpu.SMEM)


def lane_owner(shape):
    lane = lax.broadcasted_iota(jnp.int32, shape, len(shape) - 1)
    return lane // 2, lane % 2


def own_field(owner, parity, mine):
    return jnp.where(owner <= mine, 1 - parity, parity)


def sent_field(owner, parity, mine):
    return jnp.where(owner >= mine, 1 - parity, parity)


def turn_out(chosen, planes_ref, turned_ref):
    rows, latent, lanes = chosen.shape
    planes_ref[...] = chosen.reshape(rows * latent, lanes)
    for k in range(latent):
        plane = planes_ref[pl.ds(k, rows, stride=latent), :]
        turned_ref[pl.ds(k, lanes, stride=latent), :] = plane.T


def send_part(mine_ref, vectors_ref, send_ref, planes_ref, turned_ref):
    rows, _, latent, lanes = vectors_ref.shape
    owner, parity = lane_owner((1, latent, lanes))
    field = sent_field(owner, parity, mine_ref[0])
    chosen = jnp.where(
        field == 1, vectors_ref[:, 1].astype(jnp.float32), vectors_ref[:, 0].astype(jnp.float32)
    )
    turn_out(chosen, planes_ref, turned_ref)
    send_ref[...] = turned_ref[...].astype(jnp.bfloat16).reshape(send_ref.shape)


def own_part(mine_ref, vectors_ref, own_ref, planes_ref, turned_ref):
    rows, _, latent, lanes = vectors_ref.shape
    half = lanes // 2
    owner, parity = lane_owner((1, latent, lanes))
    field = own_field(owner, parity, mine_ref[0])
    chosen = jnp.where(
        field == 1, vectors_ref[:, 1].astype(jnp.float32), vectors_ref[:, 0].astype(jnp.float32)
    )
    turn_out(chosen, planes_ref, turned_ref)
    turned = turned_ref[...].reshape(half, 2, latent, rows)
    low = lax.broadcasted_iota(jnp.int32, (half, latent, rows), 0) <= mine_ref[0]
    even, odd = turned[:, 0], turned[:, 1]
    own_ref[0] = jnp.where(low, odd, even).astype(jnp.bfloat16).reshape(half * latent, rows)
    own_ref[1] = jnp.where(low, even, odd).astype(jnp.bfloat16).reshape(half * latent, rows)


def pieces(rows):
    return [pl.ds(at, min(rows, LANES)) for at in range(0, rows, LANES)]


def send_kernel(mine_ref, vectors_ref, send_ref, *scratch):
    for piece in pieces(vectors_ref.shape[0]):
        send_part(mine_ref, vectors_ref.at[piece], send_ref.at[:, :, piece], *scratch)


def own_kernel(mine_ref, vectors_ref, own_ref, *scratch):
    for piece in pieces(vectors_ref.shape[0]):
        own_part(mine_ref, vectors_ref.at[piece], own_ref.at[:, :, piece], *scratch)


def turn_call(kernel, mine, vectors, out_shape, out_block, out_map, block):
    rows, local_fields, latent, lanes = vectors.shape
    return pl.pallas_call(
        kernel,
        grid=(rows // block,),
        in_specs=[
            SMEM_SPEC,
            pl.BlockSpec((block, local_fields, latent, lanes), lambda at: (at, 0, 0, 0)),
        ],
        out_specs=pl.BlockSpec(out_block, out_map),
        out_shape=jax.ShapeDtypeStruct(out_shape, jnp.bfloat16),
        scratch_shapes=turn_scratch(block, latent, lanes),
        compiler_params=params(60),
        cost_estimate=cost(0, vectors.size * 3),
    )(mine, vectors)


def make_send(mine, vectors):
    rows, _, latent, lanes = vectors.shape
    owners, block = lanes // 2, min(rows, TURN)
    return turn_call(
        send_kernel,
        mine,
        vectors,
        (owners, 2 * latent, rows),
        (owners, 2 * latent, block),
        lambda at: (0, 0, at),
        block,
    )


def make_own(mine, vectors):
    rows, _, latent, lanes = vectors.shape
    half, block = lanes // 2, min(rows, TURN)
    return turn_call(
        own_kernel,
        mine,
        vectors,
        (2, half * latent, rows),
        (2, half * latent, block),
        lambda at: (0, 0, at),
        block,
    )


def products(mine_ref, own_ref, other_ref, first):
    slots, wide, rows = other_ref.shape
    latent = wide // 2
    others = other_ref[...].astype(jnp.float32).reshape(slots, 2, latent, rows)
    parts = []
    for i in range(2):
        part = own_ref[i].astype(jnp.float32).reshape(slots, latent, rows) * others[:, i]
        if i == 0:
            part = jnp.where(own_slot(mine_ref, part.shape, first), 0.0, part)
        parts.append(part.astype(jnp.bfloat16).reshape(slots * latent, rows))
    return parts


def own_slot(mine_ref, shape, first):
    return lax.broadcasted_iota(jnp.int32, shape, 0) + first == mine_ref[0]


def pairs_kernel(mine_ref, own_ref, other_ref, weights_ref, partial_ref):
    first, second = products(mine_ref, own_ref, other_ref, 0)
    total = jnp.dot(weights_ref[0], first, preferred_element_type=jnp.float32)
    total += jnp.dot(weights_ref[1], second, preferred_element_type=jnp.float32)
    partial_ref[...] = total.astype(jnp.bfloat16)


def make_partial(mine, own, other, weights_turned):
    _, depth, rows = own.shape
    owners, wide, _ = other.shape
    width = weights_turned.shape[1]
    block = min(rows, 512)
    return pl.pallas_call(
        pairs_kernel,
        grid=(rows // block,),
        in_specs=[
            SMEM_SPEC,
            pl.BlockSpec((2, depth, block), lambda at: (0, 0, at)),
            pl.BlockSpec((owners, wide, block), lambda at: (0, 0, at)),
            pl.BlockSpec((2, width, depth), lambda at: (0, 0, 0)),
        ],
        out_specs=pl.BlockSpec((width, block), lambda at: (0, at)),
        out_shape=jax.ShapeDtypeStruct((width, rows), jnp.bfloat16),
        compiler_params=params(24),
        cost_estimate=cost(4 * depth * rows * width, 16 * depth * rows),
    )(mine, own, other, weights_turned)


def grad_first_kernel(mine_ref, own_ref, other_ref, grad_hidden_ref, grads_ref):
    first = pl.program_id(0) * other_ref.shape[0]
    for i, pairs in enumerate(products(mine_ref, own_ref, other_ref, first)):
        grads_ref[i] = lax.dot_general(
            pairs, grad_hidden_ref[...], NT, preferred_element_type=jnp.float32
        )


def make_grad_first(mine, own, other, grad_hidden):
    _, depth, rows = own.shape
    owners, wide, _ = other.shape
    width = grad_hidden.shape[0]
    return pl.pallas_call(
        grad_first_kernel,
        grid=(CHUNKS,),
        in_specs=[
            SMEM_SPEC,
            pl.BlockSpec((2, depth // CHUNKS, rows), lambda at: (0, at, 0)),
            pl.BlockSpec((owners // CHUNKS, wide, rows), lambda at: (at, 0, 0)),
            pl.BlockSpec((width, rows), lambda at: (0, 0)),
        ],
        out_specs=pl.BlockSpec((2, depth // CHUNKS, width), lambda at: (0, at, 0)),
        out_shape=jax.ShapeDtypeStruct((2, depth, width), jnp.float32),
        compiler_params=params(60),
        cost_estimate=cost(4 * depth * rows * width, 16 * depth * rows),
    )(mine, own, other, grad_hidden)


def head_kernel(
    mine_ref,
    hidden_ref,
    second_ref,
    second_turned_ref,
    out_weight_ref,
    upstream_ref,
    weights_ref,
    own_ref,
    logits_ref,
    grad_second_ref,
    grad_out_ref,
    grad_hidden_ref,
    returning_ref,
):
    slots, wide, rows = returning_ref.shape
    latent = wide // 2

    @pl.when(pl.program_id(0) == 0)
    def _():
        hidden = hidden_ref[...].astype(jnp.float32)
        sigmoid_hidden = jax.nn.sigmoid(hidden)
        activated = (hidden * sigmoid_hidden).astype(jnp.bfloat16)
        second_pre = jnp.dot(second_turned_ref[...], activated, preferred_element_type=jnp.float32)
        sigmoid_pre = jax.nn.sigmoid(second_pre)
        second_act = second_pre * sigmoid_pre
        out_weight = out_weight_ref[:, :1]
        upstream = upstream_ref[...]
        logits_ref[...] = jnp.sum(second_act * out_weight, axis=0, keepdims=True)
        slope = sigmoid_pre * (1.0 + second_pre * (1.0 - sigmoid_pre))
        grad_pre = (upstream * out_weight * slope).astype(jnp.bfloat16)
        grad_second_ref[...] = lax.dot_general(
            activated, grad_pre, NT, preferred_element_type=jnp.float32
        )
        grad_out_ref[...] = jnp.sum(second_act * upstream, axis=1, keepdims=True)
        back_hidden = jnp.dot(second_ref[...], grad_pre, preferred_element_type=jnp.float32)
        slope = sigmoid_hidden * (1.0 + hidden * (1.0 - sigmoid_hidden))
        grad_hidden_ref[...] = (back_hidden * slope).astype(jnp.bfloat16)

    first = pl.program_id(0) * slots
    returning = []
    for i in range(2):
        grads = jnp.dot(weights_ref[i], grad_hidden_ref[...], preferred_element_type=jnp.float32)
        grads = grads.reshape(slots, latent, rows)
        if i == 0:
            grads = jnp.where(own_slot(mine_ref, grads.shape, first), 0.0, grads)
        own = own_ref[i].astype(jnp.float32).reshape(slots, latent, rows)
        returning.append(grads * own)
    returning = jnp.stack(returning, axis=1).reshape(returning_ref.shape)
    returning_ref[...] = returning.astype(jnp.bfloat16)


def run_head(
    mine, hidden, second, second_turned, out_columns, upstream, weights, own, latent
):
    width, rows = hidden.shape
    _, depth, _ = own.shape
    owners, wide = depth // latent, 2 * latent
    width_two = second.shape[1]
    fixed = lambda at: (0, 0)
    return pl.pallas_call(
        head_kernel,
        grid=(CHUNKS,),
        in_specs=[
            SMEM_SPEC,
            pl.BlockSpec((width, rows), fixed),
            pl.BlockSpec((width, width_two), fixed),
            pl.BlockSpec((width_two, width), fixed),
            pl.BlockSpec((width_two, LANES), fixed),
            pl.BlockSpec((1, rows), fixed),
            pl.BlockSpec((2, depth // CHUNKS, width), lambda at: (0, at, 0)),
            pl.BlockSpec((2, depth // CHUNKS, rows), lambda at: (0, at, 0)),
        ],
        out_specs=[
            pl.BlockSpec((1, rows), fixed),
            pl.BlockSpec((width, width_two), fixed),
            pl.BlockSpec((width_two, 1), fixed),
            pl.BlockSpec((width, rows), fixed),
            pl.BlockSpec((owners // CHUNKS, wide, rows), lambda at: (at, 0, 0)),
        ],
        out_shape=[
            jax.ShapeDtypeStruct((1, rows), jnp.float32),
            jax.ShapeDtypeStruct((width, width_two), jnp.float32),
            jax.ShapeDtypeStruct((width_two, 1), jnp.float32),
            jax.ShapeDtypeStruct((width, rows), jnp.bfloat16),
            jax.ShapeDtypeStruct((owners, wide, rows), jnp.bfloat16),
        ],
        compiler_params=params(60),
        cost_estimate=cost(4 * depth * rows * width, 24 * depth * rows),
    )(
        mine,
        hidden,
        second,
        second_turned,
        out_columns,
        upstream.reshape(1, rows),
        weights,
        own,
    )


def turn_back(rows, latent, lanes, turned_ref, planes_ref):
    turned = jnp.swapaxes(turned_ref[...].reshape(lanes, latent, rows), 0, 1)
    for k in range(latent):
        planes_ref[pl.ds(k, rows, stride=latent), :] = turned[k].T
    return planes_ref[...].reshape(rows, latent, lanes)


def own_back_part(
    mine_ref, weights_ref, grad_hidden_ref, other_ref, back_ref, planes_ref, turned_ref
):
    rows, latent, lanes = back_ref.shape
    half = lanes // 2
    shape = (half, latent, rows)
    slot = lax.broadcasted_iota(jnp.int32, shape, 0)
    low = slot <= mine_ref[0]
    others = other_ref[...].astype(jnp.float32).reshape(half, 2, latent, rows)
    grad_hidden = grad_hidden_ref[...]
    first = jnp.dot(weights_ref[0], grad_hidden, preferred_element_type=jnp.float32)
    first = jnp.where(slot == mine_ref[0], 0.0, first.reshape(shape) * others[:, 0])
    second = jnp.dot(weights_ref[1], grad_hidden, preferred_element_type=jnp.float32)
    second = second.reshape(shape) * others[:, 1]
    turned = jnp.stack([jnp.where(low, second, first), jnp.where(low, first, second)], axis=1)
    turned_ref[...] = turned.reshape(lanes * latent, rows)
    back_ref[...] = turn_back(rows, latent, lanes, turned_ref, planes_ref)


def final_part(mine_ref, back_ref, arrived_ref, grads_ref, planes_ref, turned_ref):
    rows, latent, lanes = back_ref.shape
    turned_ref[...] = arrived_ref[...].astype(jnp.float32).reshape(lanes * latent, rows)
    arrived = turn_back(rows, latent, lanes, turned_ref, planes_ref)
    owner, parity = lane_owner((1, latent, lanes))
    kept = own_field(owner, parity, mine_ref[0])
    came = sent_field(owner, parity, mine_ref[0])
    own = back_ref[...]
    for f in range(2):
        grads_ref[:, f] = jnp.where(kept == f, own, 0.0) + jnp.where(came == f, arrived, 0.0)


def own_back_kernel(mine_ref, weights_ref, grad_hidden_ref, other_ref, back_ref, *scratch):
    for piece in pieces(back_ref.shape[0]):
        own_back_part(
            mine_ref,
            weights_ref,
            grad_hidden_ref.at[:, piece],
            other_ref.at[:, :, piece],
            back_ref.at[piece],
            *scratch,
        )


def groups_of(rows):
    size = min(rows, STORE)
    return [pl.ds(at, size) for at in range(0, rows, size)]


def final_kernel(
    mine_ref,
    back_ref,
    arrived_ref,
    grads_ref,
    back_held,
    arrived_held,
    ready_ref,
    back_sems,
    arrived_sems,
    store_sems,
    *scratch,
):
    rows = back_held.shape[0]
    each = len(pieces(rows)) // len(groups_of(rows))
    arrivals, loads, stores = [], [], []
    for at, piece in enumerate(pieces(rows)):
        if at % each == 0:
            group = groups_of(rows)[at // each]
            arrivals.append(
                pltpu.make_async_copy(
                    arrived_ref.at[:, :, group],
                    arrived_held.at[:, :, group],
                    arrived_sems.at[at // each],
                )
            )
            arrivals[-1].start()
        loads.append(
            pltpu.make_async_copy(back_ref.at[piece], back_held.at[piece], back_sems.at[at])
        )
        loads[-1].start()
    for at, piece in enumerate(pieces(rows)):
        if at % each == 0:
            arrivals[at // each].wait()
        loads[at].wait()
        final_part(
            mine_ref,
            back_held.at[piece],
            arrived_held.at[:, :, piece],
            ready_ref.at[piece],
            *scratch,
        )
        stores.append(
            pltpu.make_async_copy(ready_ref.at[piece], grads_ref.at[piece], store_sems.at[at])
        )
        stores[-1].start()
    for store in stores:
        store.wait()


def turn_scratch(block, latent, lanes):
    block = min(block, LANES)
    return [
        pltpu.VMEM((block * latent, lanes), jnp.float32),
        pltpu.VMEM((lanes * latent, block), jnp.float32),
    ]


def turn_own_grads(mine, weights, grad_hidden, other):
    width, rows = grad_hidden.shape
    owners, wide, _ = other.shape
    latent, lanes, block = wide // 2, 2 * owners, min(rows, TURN)
    return pl.pallas_call(
        own_back_kernel,
        grid=(rows // block,),
        in_specs=[
            SMEM_SPEC,
            pl.BlockSpec(weights.shape, lambda at: (0, 0, 0)),
            pl.BlockSpec((width, block), lambda at: (0, at)),
            pl.BlockSpec((owners, wide, block), lambda at: (0, 0, at)),
        ],
        out_specs=pl.BlockSpec((block, latent, lanes), lambda at: (at, 0, 0)),
        out_shape=jax.ShapeDtypeStruct((rows, latent, lanes), jnp.float32),
        scratch_shapes=turn_scratch(block, latent, lanes),
        compiler_params=params(60),
        cost_estimate=cost(2 * weights.size * rows, other.size * 6),
    )(mine, weights, grad_hidden, other)


ANY_SPEC = pl.BlockSpec(memory_space=pl.ANY)


def join_grads(mine, back, arrived):
    rows, latent, lanes = back.shape
    shape = (rows, 2, latent, lanes)
    count = len(pieces(rows))
    return pl.pallas_call(
        final_kernel,
        in_specs=[SMEM_SPEC, ANY_SPEC, ANY_SPEC],
        out_specs=ANY_SPEC,
        out_shape=jax.ShapeDtypeStruct(shape, jnp.float32),
        scratch_shapes=[
            pltpu.VMEM(back.shape, jnp.float32),
            pltpu.VMEM(arrived.shape, jnp.bfloat16),
            pltpu.VMEM(shape, jnp.float32),
            pltpu.SemaphoreType.DMA((count,)),
            pltpu.SemaphoreType.DMA((len(groups_of(rows)),)),
            pltpu.SemaphoreType.DMA((count,)),
        ]
        + turn_scratch(rows, latent, lanes),
        compiler_params=params(48),
        cost_estimate=cost(0, back.size * 14),
    )(mine, back, arrived)


def inner_groups(owners):
    return [[base + at for at in range(PLANE)] for base in range(0, owners, PLANE)]


def outer_groups(owners):
    return [[base + at for base in range(0, owners, PLANE)] for at in range(PLANE)]


def exchange(blocks, groups=None):
    return lax.all_to_all(blocks, "field", 0, 0, axis_index_groups=groups, tiled=True)


def field_sum(partial):
    owners = lax.axis_size("field")
    inner, outer = inner_groups(owners), outer_groups(owners)
    depth = owners // PLANE
    units, rows = partial.shape
    share = exchange(partial.reshape(PLANE, units // PLANE, rows), inner)
    share = jnp.sum(share.astype(jnp.float32), axis=0).astype(jnp.bfloat16)
    copies = jnp.broadcast_to(share[None], (depth,) + share.shape)
    share = jnp.sum(exchange(copies, outer).astype(jnp.float32), axis=0).astype(jnp.bfloat16)
    copies = jnp.broadcast_to(share[None], (PLANE,) + share.shape)
    return exchange(copies, inner).reshape(units, rows)


def swap(value, pairs):
    return lax.ppermute(value, "batch", pairs)


def part_of(value, index, axis):
    return lax.dynamic_index_in_dim(value, index, axis, keepdims=False)


def core_share(value, core, axis):
    return part_of(value, core, axis) + swap(part_of(value, 1 - core, axis), CORE_PAIRS)


def per_device(vectors, first_weight, second_weight, out_weight, upstream):
    local_fields, half, latent, width = first_weight.shape
    mine = lax.axis_index("field").astype(jnp.int32).reshape(1)
    turned = jnp.transpose(vectors, (0, 1, 3, 2))
    weights = first_weight.reshape(local_fields, half * latent, width)
    other = exchange(make_send(mine, turned))
    out_columns = jnp.broadcast_to(out_weight[:, None], (out_weight.shape[0], LANES))
    own, second_turned, out_columns = lax.optimization_barrier(
        (make_own(mine, turned), second_weight.T, out_columns)
    )
    partial = make_partial(mine, own, other, jnp.transpose(weights, (0, 2, 1)))
    hidden = field_sum(partial)
    logits, grad_second, grad_out, grad_hidden, returning = run_head(
        mine,
        hidden,
        second_weight,
        second_turned,
        out_columns,
        upstream,
        weights,
        own,
        latent,
    )
    arrived = exchange(returning)
    place = lax.axis_index("batch")
    far, core = place // 2, place % 2
    share_first = make_grad_first(mine, own, other, grad_hidden)
    share_first = share_first.reshape(local_fields, 2, 2, half // 4, latent, width)
    share_first = core_share(share_first, core, 2)
    give_first = part_of(share_first, 1 - far, 1).astype(jnp.bfloat16)
    rows_second, width_second = grad_second.shape
    share_second = core_share(grad_second.reshape(2, rows_second // 2, width_second), core, 0)
    give_first, share_second, grad_hidden = lax.optimization_barrier(
        (give_first, share_second, grad_hidden)
    )
    take_first = swap(give_first, FAR_PAIRS)
    take_second = swap(share_second, FAR_PAIRS)
    grad_out = grad_out.reshape(-1)
    grad_out = grad_out + swap(grad_out, CORE_PAIRS)
    take_out = swap(grad_out, FAR_PAIRS)
    back = turn_own_grads(mine, weights, grad_hidden, other)
    share_first, share_second, grad_out, back = lax.optimization_barrier(
        (share_first, share_second, grad_out, back)
    )
    grad_out = grad_out + take_out
    share_second = share_second + take_second
    mate_second = swap(share_second, CORE_PAIRS)
    grad_vectors = join_grads(mine, back, arrived)
    grad_first = part_of(share_first, far, 1) + take_first.astype(jnp.float32)
    grad_second = jnp.stack(
        [
            jnp.where(core == 0, share_second, mate_second),
            jnp.where(core == 0, mate_second, share_second),
        ]
    ).reshape(rows_second, width_second)
    grad_vectors = jnp.transpose(grad_vectors, (0, 1, 3, 2))
    return (logits.reshape(-1), grad_vectors, grad_first, grad_second, grad_out)


def solution(mesh):
    return jax.shard_map(
        per_device,
        mesh=mesh,
        in_specs=(
            P("batch", "field", None, None),
            P("field", None, None, None),
            P(),
            P(),
            P("batch"),
        ),
        out_specs=(
            P("batch"),
            P("batch", "field", None, None),
            P("field", "batch", None, None),
            P(),
            P(),
        ),
        check_vma=False,
    )
```
